128 devices in a mesh: pb: 16 (over y_lo, x, core), kv: 8 (over y_hi, z).
Axes of the slice: x: 4, y: 4 (y_hi: 2, y_lo: 2; y = y_hi * 2 + y_lo), z: 4, core: 2. Of those that a mesh axis runs over, the one named last changes fastest.
Arguments:
- queries: bfloat16 [16384, 1024], P(('pb', 'kv')), may hold values from -6 to 6
- key_rows: bfloat16 [16384, 128], P(('kv', 'pb')), may hold values from -6 to 6
- value_rows: bfloat16 [16384, 128], P(('kv', 'pb')), may hold values from -0.59765625 to 0.59765625
- output: bfloat16 [16384, 1024], P(('pb', 'kv')), may hold values from -1.796875 to 1.796875
- out_grad: bfloat16 [16384, 1024], P(('pb', 'kv')), may hold values from -6 to 6
- log_norm: float32 [8, 16384], P(None, ('pb', 'kv')), as said below
- positions: int32 [16384], replicated, may hold values from 0 to 16383, as said below
Outputs:
- query_grad: float32 [16384, 1024], P(('pb', 'kv'))
- key_grad: float32 [16384, 128], P(('kv', 'pb'))
- value_grad: float32 [16384, 128], P(('kv', 'pb'))
The draws below stay inside these ranges and needn't reach their ends.
Inputs may be any that keep to these rules, and one draw needn't show every extreme that they name: A permutation of 0 to 16383: row r holds the token at position positions[r]. log_norm[h, r] - log(1 + positions[r]) lies between 0.25 and 0.75.
All inputs are finite; a program needn't handle non-finite values.
Results may differ from the reference program's by a relative error of at most 0.0041.
Values may be sent and summed in bfloat16 or wider, within the bound.
No kernel may reach another device: no remote copies, remote signals or barrier semaphores. Data moves between devices by JAX's collectives and lax.ppermute only.
A program may use at most 64 MiB of HBM per device.

```python
import math
import jax
import jax.numpy as jnp
from jax import lax

HD = 128
GROUP = 8
S = 16384
QTOK = 1024
N_PB = 16


def shared_order(key):
    return jax.random.permutation(jax.random.fold_in(key, 7), S).astype(jnp.int32)


def draw_positions(key, part):
    return shared_order(key)


def draw_log_norm(key, part):
    token_pos = shared_order(key).astype(jnp.float32)
    offset_key = jax.random.fold_in(key, 9)
    offsets = jax.random.uniform(offset_key, (GROUP, S), jnp.float32, 0.25, 0.75)
    return jnp.log(token_pos + 1.0)[None, :] + offsets


def level_of(rng, dims, pieces, low, largest):
    level, own = 1.0, jax.random.fold_in(rng, 6)
    for position, parts in pieces:
        steps = jnp.exp(jax.random.uniform(jax.random.fold_in(own, position), (parts,), jnp.float32, low / len(pieces), largest / len(pieces)))
        level = level * jnp.repeat(steps, dims[position] // parts).reshape([-1 if axis == position else 1 for axis in range(len(dims))])
    return level


def noise(key, dims, spread, bound, shards=(), held_as=jnp.bfloat16):
    entries = jax.random.normal(key, dims, jnp.float32) * spread
    if len(shards) > 0:
        entries = level_of(key, dims, shards, -0.22, 0.18) * entries
    return jnp.clip(entries, min=-bound, max=bound).astype(held_as)


def setup_inputs(seed: int = 0) -> dict:
    key_list = jax.random.split(jax.random.key(seed), 8)
    return {
        "queries": noise(key_list[0], (S, GROUP * HD), 1.0, 6.0, ((0, 128),)),
        "key_rows": noise(key_list[1], (S, HD), 1.0, 6.0, ((0, 128),)),
        "value_rows": noise(key_list[2], (S, HD), 0.1, 0.59765625, ((0, 128),)),
        "output": noise(key_list[3], (S, GROUP * HD), 0.3, 1.796875, ((0, 128),)),
        "out_grad": noise(key_list[4], (S, GROUP * HD), 1.0, 6.0, ((0, 128),)),
        "log_norm": draw_log_norm(jax.random.fold_in(key_list[7], 71), 0),
        "positions": draw_positions(jax.random.fold_in(key_list[7], 71), 0),
    }


def reference(queries, key_rows, value_rows, output, out_grad, log_norm, positions):
    inv_root = 1.0 / math.sqrt(HD)
    rows_block = math.gcd(QTOK, 256)
    inner_blocks = QTOK // rows_block
    query_all = queries.astype(jnp.float32).reshape(N_PB, inner_blocks, rows_block, GROUP, HD)
    grad_all = out_grad.astype(jnp.float32).reshape(N_PB, inner_blocks, rows_block, GROUP, HD)
    saved_all = output.astype(jnp.float32).reshape(N_PB, inner_blocks, rows_block, GROUP, HD)
    key_all = key_rows.astype(jnp.float32)
    value_all = value_rows.astype(jnp.float32)
    row_delta = lax.optimization_barrier(jnp.sum(grad_all * saved_all, axis=4))
    norm_blocks = log_norm.T.reshape(N_PB, inner_blocks, rows_block, GROUP)
    pos_blocks = positions.reshape(N_PB, inner_blocks, rows_block)

    def one_block(running, inputs):
        key_sum, value_sum = running
        query_block, grad_block, delta_block, norm_block, pos_block = inputs
        scores = jnp.einsum('tgd,cd->tgc', query_block, key_all) * inv_root
        visible = (positions[None, :] <= pos_block[:, None])[:, None, :]
        probs_full = jnp.where(visible, jnp.exp(scores - norm_block[:, :, None]), jnp.float32(0.0))
        probs_low = lax.optimization_barrier(probs_full.astype(jnp.bfloat16)).astype(jnp.float32)
        value_sum = value_sum + jnp.einsum('tgc,tgd->cd', probs_low, grad_block)
        grad_probs = jnp.einsum('tgd,cd->tgc', grad_block, value_all)
        grad_scores = probs_full * (grad_probs - delta_block[:, :, None]) * inv_root
        grad_scores = lax.optimization_barrier(grad_scores.astype(jnp.bfloat16)).astype(jnp.float32)
        query_part = jnp.einsum('tgc,cd->tgd', grad_scores, key_all).reshape(rows_block, GROUP * HD)
        key_sum = key_sum + jnp.einsum('tgc,tgd->cd', grad_scores, query_block)
        return ((key_sum, value_sum), query_part)
    empty_grad = jnp.zeros((S, HD), jnp.float32)

    def one_stripe(totals, inputs):
        key_total, value_total = totals
        (key_sum, value_sum), query_parts = lax.scan(one_block, (empty_grad, empty_grad), inputs)
        return ((key_total + key_sum, value_total + value_sum), query_parts)
    (key_total, value_total), query_parts = lax.scan(one_stripe, (empty_grad, empty_grad), (query_all, grad_all, row_delta, norm_blocks, pos_blocks))
    return (query_parts.reshape(S, GROUP * HD), key_total, value_total)
```

```python
import math

import jax
import jax.numpy as jnp
from jax import lax
from jax.experimental import pallas as pl
from jax.experimental.pallas import tpu as pltpu
from jax.sharding import Mesh, PartitionSpec as P

AXES = ("ylo", "x", "core", "yhi", "z")
SIZES = (2, 4, 2, 2, 4)
PLANE = ("yhi", "ylo", "x")
HEADS = 8
WIDTH = 128
RUN = 128
BAND = 16
BANDS = RUN // BAND
QRUNS = 4
KRUNS = 32
QROWS = QRUNS * BAND * HEADS
KROWS = KRUNS * BAND
HALF = 1024 + 32
LOG2E = math.log2(math.e)
INV_ROOT = 1.0 / math.sqrt(WIDTH)
F32 = jnp.float32
BF16 = jnp.bfloat16
HIGH = lax.Precision.HIGHEST


def rank_matrices(pos_row):
    by_lane = jnp.broadcast_to(pos_row, (RUN, RUN))
    by_row = by_lane.T
    rank_lane = jnp.sum((by_row < by_lane).astype(F32), axis=0, keepdims=True)
    row_id = lax.broadcasted_iota(jnp.int32, (RUN, RUN), 0).astype(F32)
    place = (rank_lane == row_id).astype(F32)
    return place, rank_lane


def split3(x):
    hi = x.astype(BF16)
    rest = x - hi.astype(F32)
    mid = rest.astype(BF16)
    low = (rest - mid.astype(F32)).astype(BF16)
    return hi, mid, low


def pack_rows(values, place, rank_lane):
    ordered = lax.dot_general(
        values, place, (((1,), (1,)), ((), ())), precision=HIGH, preferred_element_type=F32
    )
    pieces = []
    for band in range(BANDS):
        row = jnp.concatenate(
            [ordered[h : h + 1, band * BAND : (band + 1) * BAND] for h in range(HEADS)], axis=1
        )
        pieces.append(row)
    return jnp.concatenate(pieces, axis=0)


def prep_kernel(q_ref, g_ref, o_ref, ln_ref, k_ref, v_ref, qpos_ref, kpos_ref, pay_ref, kv_ref):
    place_q, rank_q = rank_matrices(qpos_ref[...].astype(F32))
    place_k, _ = rank_matrices(kpos_ref[...].astype(F32))
    low_q = place_q.astype(BF16)
    low_k = place_k.astype(BF16)
    q_sorted = jnp.dot(low_q, q_ref[...], preferred_element_type=F32).astype(BF16)
    g_sorted = jnp.dot(low_q, g_ref[...], preferred_element_type=F32).astype(BF16)
    for h in range(HEADS):
        for band in range(BANDS):
            at = (band * HEADS + h) * BAND
            rows = slice(band * BAND, (band + 1) * BAND)
            cols = slice(h * WIDTH, (h + 1) * WIDTH)
            pay_ref[at : at + BAND, :] = q_sorted[rows, cols]
            pay_ref[HALF + at : HALF + at + BAND, :] = g_sorted[rows, cols]
    product = g_ref[...].astype(F32) * o_ref[...].astype(F32)
    columns = [
        jnp.sum(product[:, h * WIDTH : (h + 1) * WIDTH], axis=1, keepdims=True)
        for h in range(HEADS)
    ]
    lane_id = lax.broadcasted_iota(jnp.int32, (RUN, RUN), 1)
    delta_wide = jnp.zeros((RUN, RUN), F32)
    for h in range(HEADS):
        delta_wide = jnp.where(lane_id == h, columns[h], delta_wide)
    delta = delta_wide.T[:HEADS]
    fill = jnp.zeros((BANDS, RUN), BF16)
    ln_hi, ln_mid, ln_low = split3(pack_rows(ln_ref[...] * LOG2E, place_q, rank_q))
    pay_ref[1024:1056, :] = jnp.concatenate([ln_hi, ln_mid, ln_low, fill], axis=0)
    d_hi, d_mid, d_low = split3(pack_rows(delta, place_q, rank_q))
    pay_ref[HALF + 1024 : HALF + 1056, :] = jnp.concatenate([d_hi, d_mid, d_low, fill], axis=0)
    k_sorted = jnp.dot(low_k, k_ref[...], preferred_element_type=F32).astype(BF16)
    v_sorted = jnp.dot(low_k, v_ref[...], preferred_element_type=F32).astype(BF16)
    kv = jnp.concatenate([k_sorted, v_sorted], axis=1)
    for i in range(16):
        kv_ref[i] = kv


def prep(q, g, o, ln, k, v, qpos, kpos):
    return pl.pallas_call(
        prep_kernel,
        out_shape=(
            jax.ShapeDtypeStruct((2 * HALF, WIDTH), BF16),
            jax.ShapeDtypeStruct((16, RUN, 2 * WIDTH), BF16),
        ),
        compiler_params=pltpu.CompilerParams(vmem_limit_bytes=32 * 1024 * 1024),
        name="prep",
    )(q, g, o, ln, k, v, qpos, kpos)


def sorted_kernel(pos_ref, out_ref):
    pos = pos_ref[...].astype(F32)
    rank = jnp.zeros_like(pos)
    for s in range(1, RUN):
        rank = rank + (pltpu.roll(pos, s, 1) < pos).astype(F32)
    lane = lax.broadcasted_iota(jnp.int32, pos.shape, 1).astype(F32)
    ordered = jnp.where(rank == lane, pos, 0.0)
    for s in range(1, RUN):
        ordered = ordered + jnp.where(
            pltpu.roll(rank, s, 1) == lane, pltpu.roll(pos, s, 1), 0.0
        )
    out_ref[...] = ordered


def sort_runs(pos):
    return pl.pallas_call(
        sorted_kernel, out_shape=jax.ShapeDtypeStruct(pos.shape, F32), name="sort_runs"
    )(pos)


def main_kernel(
    pos_ref, a_ref, r_ref, l_ref, oq_ref, og_ref, kva_ref, kvb_ref,
    dq_ref, dkva_ref, dkvb_ref,
    qs, gs, ks, vs, lns, ds, qps, kps, dqs, dks, dvs,
):
    for band in range(BANDS):
        rows = slice(band * RUN, (band + 1) * RUN)
        g_rows = slice(HALF + band * RUN, HALF + (band + 1) * RUN)
        for run, (qr, gr, grows) in enumerate((
            (a_ref, a_ref, g_rows), (r_ref, r_ref, g_rows),
            (l_ref, l_ref, g_rows), (oq_ref, og_ref, rows),
        )):
            at = slice(run * RUN, (run + 1) * RUN)
            qs[band, at, :] = qr[rows, :]
            gs[band, at, :] = gr[grows, :]
    for run, (qr, gr, base) in enumerate((
        (a_ref, a_ref, HALF), (r_ref, r_ref, HALF), (l_ref, l_ref, HALF), (oq_ref, og_ref, 0),
    )):
        ln3 = qr[1024:1056, :].astype(F32)
        d3 = gr[base + 1024 : base + 1056, :].astype(F32)
        lns[:, run * RUN : (run + 1) * RUN] = (ln3[16:24] + ln3[8:16]) + ln3[0:8]
        ds[:, run * RUN : (run + 1) * RUN] = (d3[16:24] + d3[8:16]) + d3[0:8]
        row = pos_ref[KRUNS + run : KRUNS + run + 1, :]
        for band in range(BANDS):
            piece = row[:, band * BAND : (band + 1) * BAND]
            qps[band : band + 1, run * RUN : (run + 1) * RUN] = jnp.concatenate(
                [piece] * HEADS, axis=1
            )
    key_pos = pos_ref[0:KRUNS, :].T
    for run in range(KRUNS):
        ref = kva_ref if run < 16 else kvb_ref
        for band in range(BANDS):
            rows = slice(band * BAND, (band + 1) * BAND)
            at = slice(run * BAND, (run + 1) * BAND)
            ks[band, at, :] = ref[run % 16, rows, :WIDTH]
            vs[band, at, :] = ref[run % 16, rows, WIDTH:]
            kps[band, at, :] = jnp.broadcast_to(key_pos[rows, run : run + 1], (BAND, WIDTH))
    dqs[...] = jnp.zeros_like(dqs)
    dks[...] = jnp.zeros_like(dks)
    dvs[...] = jnp.zeros_like(dvs)

    def key_band(t, carry):
        key = ks[t]
        value = vs[t]
        first_key = jnp.min(kps[t])

        def query_band(u, inner):
            @pl.when(jnp.max(qps[pl.ds(u, 1), :]) >= first_key)
            def _():
                q = qs[u]
                g = gs[u]
                scores = lax.dot_general(
                    key, q, (((1,), (1,)), ((), ())), preferred_element_type=F32
                )
                ln = lns[pl.ds(u, 1), :]
                visible = kps[t][:, 0:1] <= qps[pl.ds(u, 1), :]
                probs = jnp.where(visible, jnp.exp2(scores * (INV_ROOT * LOG2E) - ln), 0.0)
                dvs[t] += jnp.dot(probs.astype(BF16), g, preferred_element_type=F32)
                grad_probs = lax.dot_general(
                    value, g, (((1,), (1,)), ((), ())), preferred_element_type=F32
                )
                grad_scores = (probs * (grad_probs - ds[pl.ds(u, 1), :])).astype(BF16)
                dks[t] += jnp.dot(grad_scores, q, preferred_element_type=F32)
                dqs[u] += lax.dot_general(
                    grad_scores, key, (((0,), (0,)), ((), ())), preferred_element_type=F32
                )

            return inner

        return lax.fori_loop(0, BANDS, query_band, carry)

    lax.fori_loop(0, BANDS, key_band, 0)

    for band in range(BANDS):
        for run in range(QRUNS):
            dq_ref[run, band * RUN : (band + 1) * RUN, :] = (
                dqs[band, run * RUN : (run + 1) * RUN, :] * INV_ROOT
            ).astype(BF16)
    for run in range(KRUNS):
        ref = dkva_ref if run < 16 else dkvb_ref
        for band in range(BANDS):
            rows = slice(band * BAND, (band + 1) * BAND)
            at = slice(run * BAND, (run + 1) * BAND)
            ref[run % 16, rows, :WIDTH] = (dks[band, at, :] * INV_ROOT).astype(BF16)
            ref[run % 16, rows, WIDTH:] = dvs[band, at, :].astype(BF16)


def main(pos, a, r, l, oq, og, kva, kvb):
    return pl.pallas_call(
        main_kernel,
        out_shape=(
            jax.ShapeDtypeStruct((QRUNS, 1024, WIDTH), BF16),
            jax.ShapeDtypeStruct((16, RUN, 2 * WIDTH), BF16),
            jax.ShapeDtypeStruct((16, RUN, 2 * WIDTH), BF16),
        ),
        scratch_shapes=[
            pltpu.VMEM((BANDS, QROWS, WIDTH), BF16),
            pltpu.VMEM((BANDS, QROWS, WIDTH), BF16),
            pltpu.VMEM((BANDS, KROWS, WIDTH), BF16),
            pltpu.VMEM((BANDS, KROWS, WIDTH), BF16),
            pltpu.VMEM((BANDS, QROWS), F32),
            pltpu.VMEM((BANDS, QROWS), F32),
            pltpu.VMEM((BANDS, QROWS), F32),
            pltpu.VMEM((BANDS, KROWS, WIDTH), F32),
            pltpu.VMEM((BANDS, QROWS, WIDTH), F32),
            pltpu.VMEM((BANDS, KROWS, WIDTH), F32),
            pltpu.VMEM((BANDS, KROWS, WIDTH), F32),
        ],
        compiler_params=pltpu.CompilerParams(vmem_limit_bytes=56 * 1024 * 1024),
        name="block_grads",
    )(pos, a, r, l, oq, og, kva, kvb)


def query_kernel(own_ref, b_ref, c_ref, d_ref, pos_ref, out_ref):
    place, _ = rank_matrices(pos_ref[...].astype(F32))
    total = (
        own_ref[...].astype(F32) + b_ref[...].astype(F32)
        + c_ref[...].astype(F32) + d_ref[...].astype(F32)
    ).reshape(BANDS, HEADS, BAND, WIDTH)
    for h in range(HEADS):
        out_ref[:, h * WIDTH : (h + 1) * WIDTH] = lax.dot_general(
            place, total[:, h].reshape(RUN, WIDTH), (((0,), (0,)), ((), ())),
            precision=HIGH, preferred_element_type=F32,
        )


def key_kernel(parts_ref, pos_ref, dk_ref, dv_ref):
    place, _ = rank_matrices(pos_ref[...].astype(F32))
    total = parts_ref[0].astype(F32)
    for i in range(1, 16):
        total = total + parts_ref[i].astype(F32)
    result = lax.dot_general(
        place, total, (((0,), (0,)), ((), ())), precision=HIGH, preferred_element_type=F32
    )
    dk_ref[...] = result[:, :WIDTH]
    dv_ref[...] = result[:, WIDTH:]


def shards(queries, key_rows, value_rows, output, out_grad, log_norm, positions):
    ylo, x, core, yhi, z = (lax.axis_index(name) for name in AXES)
    pb = (ylo * 4 + x) * 2 + core
    q_block = pb * 8 + yhi * 4 + z
    k_block = (yhi * 4 + z) * 16 + pb
    pos = positions.reshape(128, RUN)
    qpos = lax.dynamic_slice_in_dim(pos, q_block, 1)
    kpos = lax.dynamic_slice_in_dim(pos, k_block, 1)
    payload, kv_out = prep(
        queries, out_grad, output, log_norm, key_rows, value_rows, qpos, kpos
    )

    def along_z(array, step):
        return lax.ppermute(array, "z", [(i, (i + step) % 4) for i in range(4)])

    from_left = along_z(payload, 1)
    from_right = along_z(payload, 3)
    far_q = along_z(from_left[:HALF], 1)
    far_g = along_z(from_right[HALF:], 3)
    kv_mine = lax.all_to_all(kv_out, PLANE, 0, 0, tiled=True)
    kv_other = lax.ppermute(kv_mine, "core", [(0, 1), (1, 0)])

    plane = pos.reshape(2, 4, 2, 4, 2, RUN)
    plane = lax.dynamic_slice_in_dim(plane, z, 1, axis=1)[:, 0]
    mine = lax.dynamic_slice_in_dim(plane, core, 1, axis=3).reshape(16, RUN)
    other = lax.dynamic_slice_in_dim(plane, 1 - core, 1, axis=3).reshape(16, RUN)
    line = lax.dynamic_slice_in_dim(pos, q_block - z, 4)
    line = jnp.concatenate([line, line], axis=0)
    line = lax.dynamic_slice_in_dim(line, z, 4)
    line = jnp.stack([line[0], line[3], line[1], line[2]])
    runs = sort_runs(jnp.concatenate([mine, other, line, line], axis=0))

    dq, dkv_mine, dkv_other = main(
        runs, payload, from_left, from_right, far_q, far_g, kv_mine, kv_other
    )
    dq_left = along_z(dq[1], 3)
    dq_right = along_z(dq[2], 1)
    dq_far = along_z(dq[3], 2)
    dkv_in = lax.ppermute(dkv_other, "core", [(0, 1), (1, 0)])
    dkv_sum = (dkv_mine.astype(F32) + dkv_in.astype(F32)).astype(BF16)
    dkv_parts = lax.all_to_all(dkv_sum, PLANE, 0, 0, tiled=True)
    query_grad = pl.pallas_call(
        query_kernel, out_shape=jax.ShapeDtypeStruct((RUN, HEADS * WIDTH), F32), name="query_sum",
        compiler_params=pltpu.CompilerParams(vmem_limit_bytes=32 * 1024 * 1024),
    )(dq[0], dq_left, dq_right, dq_far, qpos)
    key_grad, value_grad = pl.pallas_call(
        key_kernel,
        out_shape=(
            jax.ShapeDtypeStruct((RUN, WIDTH), F32),
            jax.ShapeDtypeStruct((RUN, WIDTH), F32),
        ),
        name="key_sum",
        compiler_params=pltpu.CompilerParams(vmem_limit_bytes=32 * 1024 * 1024),
    )(dkv_parts, kpos)
    return query_grad, key_grad, value_grad


def solution(mesh):
    fine = Mesh(mesh.devices.reshape(SIZES), AXES)
    by_query = P(AXES, None)
    by_key = P(("yhi", "z", "ylo", "x", "core"), None)
    return jax.shard_map(
        shards,
        mesh=fine,
        in_specs=(by_query, by_key, by_key, by_query, by_query, P(None, AXES), P()),
        out_specs=(by_query, by_key, by_key),
        check_vma=False,
    )
```

```python
import math

import jax
import jax.numpy as jnp
from jax import lax
from jax.experimental import pallas as pl
from jax.experimental.pallas import tpu as pltpu
from jax.sharding import Mesh, PartitionSpec as P

AXES = ("ylo", "x", "core", "yhi", "z")
SIZES = (2, 4, 2, 2, 4)
PLANE = ("yhi", "ylo", "x")
HEADS = 8
WIDTH = 128
RUN = 128
BAND = 16
BANDS = RUN // BAND
QRUNS = 8
KRUNS = 16
QROWS = QRUNS * BAND * HEADS
KROWS = KRUNS * BAND
MERGE = 4
PART = 256
PCOL = 256
HALF = 1024 + 32
LOG2E = math.log2(math.e)
INV_ROOT = 1.0 / math.sqrt(WIDTH)
F32 = jnp.float32
BF16 = jnp.bfloat16
HIGH = lax.Precision.HIGHEST


def rank_matrices(pos_row):
    by_lane = jnp.broadcast_to(pos_row, (RUN, RUN))
    by_row = by_lane.T
    rank_lane = jnp.sum((by_row < by_lane).astype(F32), axis=0, keepdims=True)
    row_id = lax.broadcasted_iota(jnp.int32, (RUN, RUN), 0).astype(F32)
    place = (rank_lane == row_id).astype(F32)
    return place, rank_lane


def split3(x):
    hi = x.astype(BF16)
    rest = x - hi.astype(F32)
    mid = rest.astype(BF16)
    low = (rest - mid.astype(F32)).astype(BF16)
    return hi, mid, low


def pack_rows(values, place, rank_lane):
    ordered = lax.dot_general(
        values, place, (((1,), (1,)), ((), ())), precision=HIGH, preferred_element_type=F32
    )
    pieces = []
    for band in range(BANDS):
        row = jnp.concatenate(
            [ordered[h : h + 1, band * BAND : (band + 1) * BAND] for h in range(HEADS)], axis=1
        )
        pieces.append(row)
    return jnp.concatenate(pieces, axis=0)


def placed(index):
    ylo, x, core, yhi, z = index
    pb = (ylo * 4 + x) * 2 + core
    return pb * 8 + yhi * 4 + z, (yhi * 4 + z) * 16 + pb


def own_index():
    return tuple(lax.axis_index(name) for name in AXES)


def prep_kernel(
    q_hbm, g_hbm, o_hbm, ln_hbm, k_hbm, v_hbm, pos_hbm, pay_ref, kv_ref,
    q_ref, g_ref, o_ref, ln_ref, k_ref, v_ref, pos_ref, sems,
):
    copies = [
        pltpu.make_async_copy(src, dst, sems.at[i])
        for i, (src, dst) in enumerate((
            (pos_hbm, pos_ref), (k_hbm, k_ref), (v_hbm, v_ref), (q_hbm, q_ref),
            (g_hbm, g_ref), (o_hbm, o_ref), (ln_hbm, ln_ref),
        ))
    ]
    for copy in copies:
        copy.start()
    for copy in copies:
        copy.wait()
    q_block, k_block = placed(own_index())
    place_q, rank_q = rank_matrices(pos_ref[pl.ds(q_block, 1), :].astype(F32))
    place_k, _ = rank_matrices(pos_ref[pl.ds(k_block, 1), :].astype(F32))
    low_q = place_q.astype(BF16)
    low_k = place_k.astype(BF16)
    q_sorted = jnp.dot(low_q, q_ref[...], preferred_element_type=F32).astype(BF16)
    g_sorted = jnp.dot(low_q, g_ref[...], preferred_element_type=F32).astype(BF16)
    for h in range(HEADS):
        for band in range(BANDS):
            at = (band * HEADS + h) * BAND
            rows = slice(band * BAND, (band + 1) * BAND)
            cols = slice(h * WIDTH, (h + 1) * WIDTH)
            pay_ref[at : at + BAND, :] = q_sorted[rows, cols]
            pay_ref[HALF + at : HALF + at + BAND, :] = g_sorted[rows, cols]
    product = g_ref[...].astype(F32) * o_ref[...].astype(F32)
    columns = [
        jnp.sum(product[:, h * WIDTH : (h + 1) * WIDTH], axis=1, keepdims=True)
        for h in range(HEADS)
    ]
    lane_id = lax.broadcasted_iota(jnp.int32, (RUN, RUN), 1)
    delta_wide = jnp.zeros((RUN, RUN), F32)
    for h in range(HEADS):
        delta_wide = jnp.where(lane_id == h, columns[h], delta_wide)
    delta = delta_wide.T[:HEADS]
    fill = jnp.zeros((BANDS, RUN), BF16)
    ln_hi, ln_mid, ln_low = split3(pack_rows(ln_ref[...] * (-1.0 / INV_ROOT), place_q, rank_q))
    pay_ref[1024:1056, :] = jnp.concatenate([ln_hi, ln_mid, ln_low, fill], axis=0)
    d_hi, d_mid, d_low = split3(pack_rows(-delta, place_q, rank_q))
    pay_ref[HALF + 1024 : HALF + 1056, :] = jnp.concatenate([d_hi, d_mid, d_low, fill], axis=0)
    k_sorted = jnp.dot(low_k, k_ref[...], preferred_element_type=F32).astype(BF16)
    v_sorted = jnp.dot(low_k, v_ref[...], preferred_element_type=F32).astype(BF16)
    kv = jnp.concatenate([k_sorted, v_sorted], axis=1)
    for i in range(16):
        kv_ref[i] = kv


def prep(q, g, o, ln, k, v, pos):
    return pl.pallas_call(
        prep_kernel,
        in_specs=[pl.BlockSpec(memory_space=pl.ANY)] * 7,
        out_shape=(
            jax.ShapeDtypeStruct((2 * HALF, WIDTH), BF16),
            jax.ShapeDtypeStruct((16, RUN, 2 * WIDTH), BF16),
        ),
        scratch_shapes=[
            pltpu.VMEM((RUN, HEADS * WIDTH), BF16),
            pltpu.VMEM((RUN, HEADS * WIDTH), BF16),
            pltpu.VMEM((RUN, HEADS * WIDTH), BF16),
            pltpu.VMEM((HEADS, RUN), F32),
            pltpu.VMEM((RUN, WIDTH), BF16),
            pltpu.VMEM((RUN, WIDTH), BF16),
            pltpu.VMEM((128, RUN), jnp.int32),
            pltpu.SemaphoreType.DMA((7,)),
        ],
        compiler_params=pltpu.CompilerParams(vmem_limit_bytes=60 * 1024 * 1024),
        name="prep",
    )(q, g, o, ln, k, v, pos)


def sorted_kernel(pos_ref, out_ref):
    ylo, x, core, yhi, z = own_index()
    rows = []
    for key_yhi in range(2):
        for key_ylo in range(2):
            for key_x in range(4):
                rows.append(placed((key_ylo, key_x, core, key_yhi, z))[1])
    for query_core in (core, 1 - core):
        for query_z in (z, (z + 3) % 4, (z + 1) % 4, (z + 2) % 4):
            rows.append(placed((ylo, x, query_core, yhi, query_z))[0])
    pos = jnp.concatenate([pos_ref[pl.ds(row, 1), :] for row in rows], axis=0).astype(F32)
    rank = jnp.zeros_like(pos)
    for s in range(1, RUN):
        rank = rank + (pltpu.roll(pos, s, 1) < pos).astype(F32)
    lane = lax.broadcasted_iota(jnp.int32, pos.shape, 1).astype(F32)
    ordered = jnp.where(rank == lane, pos, 0.0)
    for s in range(1, RUN):
        ordered = ordered + jnp.where(
            pltpu.roll(rank, s, 1) == lane, pltpu.roll(pos, s, 1), 0.0
        )
    out_ref[...] = ordered


def sort_runs(pos):
    return pl.pallas_call(
        sorted_kernel,
        out_shape=jax.ShapeDtypeStruct((KRUNS + QRUNS, RUN), F32),
        name="sort_runs",
    )(pos)


def main_kernel(*refs):
    pos_ref, spos = refs[:2]
    runs = refs[2:10]
    kv_ref = refs[10]
    dq_near, dq_own, dq_other, dkv_ref = refs[11:15]
    qpt, kps, dqs, dks, dvs, tx, kx, vx = refs[15:]
    for run, pay in enumerate(runs):
        terms = jnp.concatenate(
            [
                pay[1024:1056, :].astype(F32),
                pay[HALF + 1024 : HALF + 1056, :].astype(F32),
                jnp.zeros((RUN - 64, RUN), F32),
            ],
            axis=0,
        )
        tx[run * RUN : (run + 1) * RUN, :] = terms.T.astype(BF16)
    query_pos = pos_ref[KRUNS : KRUNS + QRUNS, :].T
    lane = lax.broadcasted_iota(jnp.int32, (BAND, WIDTH), 1)
    for band in range(BANDS):
        rows = slice(band * BAND, (band + 1) * BAND)
        kx[band] = ((lane % 8 == band) & (lane < 24)).astype(F32).astype(BF16)
        vx[band] = ((lane % 8 == band) & (lane >= 32) & (lane < 56)).astype(F32).astype(BF16)
        for run in range(QRUNS):
            qpt[band, run * BAND : (run + 1) * BAND, :] = jnp.broadcast_to(
                query_pos[rows, run : run + 1], (BAND, WIDTH)
            )
        kps[band : band + 1, :] = jnp.concatenate(
            [pos_ref[run : run + 1, rows] for run in range(KRUNS)], axis=1
        )
    dks[...] = jnp.zeros_like(dks)
    dvs[...] = jnp.zeros_like(dvs)
    by_cols = (((1,), (1,)), ((), ()))
    by_rows = (((0,), (0,)), ((), ()))

    def block(u, first, bands):
        at = pl.ds(pl.multiple_of(u * RUN, RUN), RUN)
        g_at = pl.ds(pl.multiple_of(HALF + u * RUN, 16), RUN)
        q = jnp.concatenate([pay[at, :] for pay in runs], axis=0)
        g = jnp.concatenate([pay[g_at, :] for pay in runs], axis=0)
        terms = tx[...]
        rows = [
            pl.ds(pl.multiple_of((first + i) * BAND, BAND), BAND) for i in range(bands)
        ]
        key = jnp.concatenate(
            [kv_ref[run, r, :WIDTH] for r in rows for run in range(KRUNS)], axis=0
        )
        value = jnp.concatenate(
            [kv_ref[run, r, WIDTH:] for r in rows for run in range(KRUNS)], axis=0
        )
        key_pick = jnp.concatenate([kx[u]] * (KRUNS * bands), axis=0)
        value_pick = jnp.concatenate([vx[u]] * (KRUNS * bands), axis=0)
        q_terms = jnp.concatenate([q, terms], axis=1)
        g_terms = jnp.concatenate([g, terms], axis=1)
        key_terms = jnp.concatenate([key, key_pick], axis=1)
        value_terms = jnp.concatenate([value, value_pick], axis=1)
        wide = KROWS * bands
        key_pos = jnp.concatenate([kps[pl.ds(first + i, 1), :] for i in range(bands)], axis=1)
        probs_low, grads_low = [], []
        for part in range(QROWS // PART):
            mine = slice(part * PART, (part + 1) * PART)
            lows = []
            for c in range(0, wide, PCOL):
                cs = slice(c, c + PCOL)
                scores = lax.dot_general(
                    q_terms[mine], key_terms[cs], by_cols, preferred_element_type=F32
                )
                grad_probs = lax.dot_general(
                    g_terms[mine], value_terms[cs], by_cols, preferred_element_type=F32
                )
                column = jnp.concatenate(
                    [
                        qpt[u, run * BAND : (run + 1) * BAND, :]
                        for run in range(part * PART // RUN, ((part + 1) * PART + RUN - 1) // RUN)
                        for _ in range(min(PART, RUN) // BAND)
                    ],
                    axis=0,
                )
                visible = key_pos[:, cs] <= jnp.concatenate([column] * (PCOL // WIDTH), axis=1)
                probs = jnp.where(visible, jnp.exp2(scores * (INV_ROOT * LOG2E)), 0.0)
                lows.append((probs.astype(BF16), (probs * grad_probs).astype(BF16)))
            probs_low.append(jnp.concatenate([x[0] for x in lows], axis=1))
            grads_low.append(jnp.concatenate([x[1] for x in lows], axis=1))
        probs_low = jnp.concatenate(probs_low, axis=0)
        grad_scores = jnp.concatenate(grads_low, axis=0)
        dv = lax.dot_general(g, probs_low, by_rows, preferred_element_type=F32)
        dk = lax.dot_general(q, grad_scores, by_rows, preferred_element_type=F32)
        for i in range(bands):
            cols = slice(i * KROWS, (i + 1) * KROWS)
            dvs[first + i] += dv[:, cols]
            dks[first + i] += dk[:, cols]
        dqs[...] += jnp.dot(grad_scores, key, preferred_element_type=F32)

    def query_band(u, carry):
        last = spos[KRUNS, u * BAND + BAND - 1]
        for run in range(1, QRUNS):
            last = jnp.maximum(last, spos[KRUNS + run, u * BAND + BAND - 1])
        seen = 0
        for t in range(BANDS):
            first = spos[0, t * BAND]
            for run in range(1, KRUNS):
                first = jnp.minimum(first, spos[run, t * BAND])
            seen = seen + jnp.where(last >= first, 1, 0)
        dqs[...] = jnp.zeros_like(dqs)
        done = lax.div(seen, MERGE) * MERGE

        def many(j, carry):
            block(u, j * MERGE, MERGE)
            return carry

        lax.fori_loop(0, lax.div(seen, MERGE), many, 0)

        def single(j, carry):
            block(u, j, 1)
            return carry

        lax.fori_loop(done, seen, single, 0)
        rows = pl.ds(pl.multiple_of(u * RUN, RUN), RUN)
        dq_near[rows, :] = dqs[0:RUN, :] * INV_ROOT
        for run in range(1, 4):
            dq_own[run - 1, rows, :] = dqs[run * RUN : (run + 1) * RUN, :] * INV_ROOT
        for run in range(4):
            dq_other[run, rows, :] = (
                dqs[(4 + run) * RUN : (5 + run) * RUN, :] * INV_ROOT
            ).astype(BF16)
        return carry

    lax.fori_loop(0, BANDS, query_band, 0)
    for band in range(BANDS):
        rows = slice(band * BAND, (band + 1) * BAND)
        key_part = (dks[band] * INV_ROOT).T.astype(BF16)
        value_part = dvs[band].T.astype(BF16)
        for run in range(KRUNS):
            dkv_ref[run, rows, :WIDTH] = key_part[run * BAND : (run + 1) * BAND]
            dkv_ref[run, rows, WIDTH:] = value_part[run * BAND : (run + 1) * BAND]


def main(runs, payloads, kv):
    vmem = pl.BlockSpec(memory_space=pltpu.VMEM)
    return pl.pallas_call(
        main_kernel,
        in_specs=[vmem, pl.BlockSpec(memory_space=pltpu.SMEM)] + [vmem] * 9,
        out_shape=(
            jax.ShapeDtypeStruct((1024, WIDTH), F32),
            jax.ShapeDtypeStruct((3, 1024, WIDTH), F32),
            jax.ShapeDtypeStruct((4, 1024, WIDTH), BF16),
            jax.ShapeDtypeStruct((16, RUN, 2 * WIDTH), BF16),
        ),
        scratch_shapes=[
            pltpu.VMEM((BANDS, QRUNS * BAND, WIDTH), F32),
            pltpu.VMEM((BANDS, KROWS), F32),
            pltpu.VMEM((QROWS, WIDTH), F32),
            pltpu.VMEM((BANDS, WIDTH, KROWS), F32),
            pltpu.VMEM((BANDS, WIDTH, KROWS), F32),
            pltpu.VMEM((QROWS, WIDTH), BF16),
            pltpu.VMEM((BANDS, BAND, WIDTH), BF16),
            pltpu.VMEM((BANDS, BAND, WIDTH), BF16),
        ],
        compiler_params=pltpu.CompilerParams(vmem_limit_bytes=56 * 1024 * 1024),
        name="block_grads",
    )(runs, runs, *payloads, kv)


def query_kernel(own_ref, in_ref, b_ref, c_ref, d_ref, pos_ref, out_ref):
    q_block, _ = placed(own_index())
    place, _ = rank_matrices(pos_ref[pl.ds(q_block, 1), :].astype(F32))
    total = own_ref[...] + in_ref[0].astype(F32)
    for ref in (b_ref, c_ref, d_ref):
        total = total + ref[...].astype(F32)
    total = total.reshape(BANDS, HEADS, BAND, WIDTH)
    for h in range(HEADS):
        out_ref[:, h * WIDTH : (h + 1) * WIDTH] = lax.dot_general(
            place, total[:, h].reshape(RUN, WIDTH), (((0,), (0,)), ((), ())),
            precision=HIGH, preferred_element_type=F32,
        )


def key_kernel(parts_ref, pos_ref, dk_ref, dv_ref):
    _, k_block = placed(own_index())
    place, _ = rank_matrices(pos_ref[pl.ds(k_block, 1), :].astype(F32))
    total = parts_ref[0].astype(F32)
    for i in range(1, 16):
        total = total + parts_ref[i].astype(F32)
    result = lax.dot_general(
        place, total, (((0,), (0,)), ((), ())), precision=HIGH, preferred_element_type=F32
    )
    dk_ref[...] = result[:, :WIDTH]
    dv_ref[...] = result[:, WIDTH:]


def shards(queries, key_rows, value_rows, output, out_grad, log_norm, positions):
    pos = positions.reshape(128, RUN)
    payload, kv_out = prep(queries, out_grad, output, log_norm, key_rows, value_rows, pos)

    def along_z(array, step):
        return lax.ppermute(array, "z", [(i, (i + step) % 4) for i in range(4)])

    def cross(array):
        return lax.ppermute(array, "core", [(0, 1), (1, 0)])

    from_left = along_z(payload, 1)
    from_right = along_z(payload, 3)
    from_far = along_z(payload, 2)
    mine = (payload, from_left, from_right, from_far)
    payloads = mine + tuple(cross(array) for array in mine)
    kv = lax.all_to_all(kv_out, PLANE, 0, 0, tiled=True)
    dq_near, dq_own, dq_other, dkv = main(sort_runs(pos), payloads, kv)
    dkv_parts = lax.all_to_all(dkv, PLANE, 0, 0, tiled=True)
    dq_in = cross(dq_other)
    dq_sum = (dq_own + dq_in[1:].astype(F32)).astype(BF16)
    dq_left = along_z(dq_sum[0], 3)
    dq_right = along_z(dq_sum[1], 1)
    dq_far = along_z(dq_sum[2], 2)
    query_grad = pl.pallas_call(
        query_kernel, out_shape=jax.ShapeDtypeStruct((RUN, HEADS * WIDTH), F32), name="query_sum",
        compiler_params=pltpu.CompilerParams(vmem_limit_bytes=32 * 1024 * 1024),
    )(dq_near, dq_in, dq_left, dq_right, dq_far, pos)
    key_grad, value_grad = pl.pallas_call(
        key_kernel,
        out_shape=(
            jax.ShapeDtypeStruct((RUN, WIDTH), F32),
            jax.ShapeDtypeStruct((RUN, WIDTH), F32),
        ),
        name="key_sum",
        compiler_params=pltpu.CompilerParams(vmem_limit_bytes=32 * 1024 * 1024),
    )(dkv_parts, pos)
    return query_grad, key_grad, value_grad


def solution(mesh):
    fine = Mesh(mesh.devices.reshape(SIZES), AXES)
    by_query = P(AXES, None)
    by_key = P(("yhi", "z", "ylo", "x", "core"), None)
    return jax.shard_map(
        shards,
        mesh=fine,
        in_specs=(by_query, by_key, by_key, by_query, by_query, P(None, AXES), P()),
        out_specs=(by_query, by_key, by_key),
        check_vma=False,
    )
```

```python
import math

import jax
import jax.numpy as jnp
from jax import lax
from jax.experimental import pallas as pl
from jax.experimental.pallas import tpu as pltpu
from jax.sharding import Mesh, PartitionSpec as P

AXES = ("ylo", "x", "core", "yhi", "z")
SIZES = (2, 4, 2, 2, 4)
PLANE = ("yhi", "ylo", "x")
HEADS = 8
WIDTH = 128
RUN = 128
BAND = 16
BANDS = RUN // BAND
QRUNS = 8
KRUNS = 16
QROWS = QRUNS * BAND * HEADS
KROWS = KRUNS * BAND
MERGE = 4
PART = 256
PCOL = 256
HALF = 1024 + 32
LOG2E = math.log2(math.e)
INV_ROOT = 1.0 / math.sqrt(WIDTH)
F32 = jnp.float32
BF16 = jnp.bfloat16
HIGH = lax.Precision.HIGHEST


def rank_matrices(pos_row):
    by_lane = jnp.broadcast_to(pos_row, (RUN, RUN))
    by_row = by_lane.T
    rank_lane = jnp.sum((by_row < by_lane).astype(F32), axis=0, keepdims=True)
    row_id = lax.broadcasted_iota(jnp.int32, (RUN, RUN), 0).astype(F32)
    place = (rank_lane == row_id).astype(F32)
    return place, rank_lane


def split3(x):
    hi = x.astype(BF16)
    rest = x - hi.astype(F32)
    mid = rest.astype(BF16)
    low = (rest - mid.astype(F32)).astype(BF16)
    return hi, mid, low


def pack_rows(values, place, rank_lane):
    ordered = lax.dot_general(
        values, place, (((1,), (1,)), ((), ())), precision=HIGH, preferred_element_type=F32
    )
    pieces = []
    for band in range(BANDS):
        row = jnp.concatenate(
            [ordered[h : h + 1, band * BAND : (band + 1) * BAND] for h in range(HEADS)], axis=1
        )
        pieces.append(row)
    return jnp.concatenate(pieces, axis=0)


def placed(index):
    ylo, x, core, yhi, z = index
    pb = (ylo * 4 + x) * 2 + core
    return pb * 8 + yhi * 4 + z, (yhi * 4 + z) * 16 + pb


def own_index():
    return tuple(lax.axis_index(name) for name in AXES)


def prep_kernel(
    q_hbm, g_hbm, o_hbm, ln_hbm, k_hbm, v_hbm, pos_hbm, pay_ref, kv_ref,
    q_ref, g_ref, o_ref, ln_ref, k_ref, v_ref, pos_ref, sems,
):
    copies = [
        pltpu.make_async_copy(src, dst, sems.at[i])
        for i, (src, dst) in enumerate((
            (pos_hbm, pos_ref), (k_hbm, k_ref), (v_hbm, v_ref), (q_hbm, q_ref),
            (g_hbm, g_ref), (o_hbm, o_ref), (ln_hbm, ln_ref),
        ))
    ]
    for copy in copies:
        copy.start()
    for copy in copies:
        copy.wait()
    q_block, k_block = placed(own_index())
    place_q, rank_q = rank_matrices(pos_ref[pl.ds(q_block, 1), :].astype(F32))
    place_k, _ = rank_matrices(pos_ref[pl.ds(k_block, 1), :].astype(F32))
    low_q = place_q.astype(BF16)
    low_k = place_k.astype(BF16)
    q_sorted = jnp.dot(low_q, q_ref[...], preferred_element_type=F32).astype(BF16)
    g_sorted = jnp.dot(low_q, g_ref[...], preferred_element_type=F32).astype(BF16)
    for h in range(HEADS):
        for band in range(BANDS):
            at = (band * HEADS + h) * BAND
            rows = slice(band * BAND, (band + 1) * BAND)
            cols = slice(h * WIDTH, (h + 1) * WIDTH)
            pay_ref[at : at + BAND, :] = q_sorted[rows, cols]
            pay_ref[HALF + at : HALF + at + BAND, :] = g_sorted[rows, cols]
    product = g_ref[...].astype(F32) * o_ref[...].astype(F32)
    columns = [
        jnp.sum(product[:, h * WIDTH : (h + 1) * WIDTH], axis=1, keepdims=True)
        for h in range(HEADS)
    ]
    lane_id = lax.broadcasted_iota(jnp.int32, (RUN, RUN), 1)
    delta_wide = jnp.zeros((RUN, RUN), F32)
    for h in range(HEADS):
        delta_wide = jnp.where(lane_id == h, columns[h], delta_wide)
    delta = delta_wide.T[:HEADS]
    fill = jnp.zeros((BANDS, RUN), BF16)
    ln_hi, ln_mid, ln_low = split3(pack_rows(ln_ref[...] * (-1.0 / INV_ROOT), place_q, rank_q))
    pay_ref[1024:1056, :] = jnp.concatenate([ln_hi, ln_mid, ln_low, fill], axis=0)
    d_hi, d_mid, d_low = split3(pack_rows(-delta, place_q, rank_q))
    pay_ref[HALF + 1024 : HALF + 1056, :] = jnp.concatenate([d_hi, d_mid, d_low, fill], axis=0)
    k_sorted = jnp.dot(low_k, k_ref[...], preferred_element_type=F32).astype(BF16)
    v_sorted = jnp.dot(low_k, v_ref[...], preferred_element_type=F32).astype(BF16)
    kv = jnp.concatenate([k_sorted, v_sorted], axis=1)
    for i in range(16):
        kv_ref[i] = kv


def prep(q, g, o, ln, k, v, pos):
    return pl.pallas_call(
        prep_kernel,
        in_specs=[pl.BlockSpec(memory_space=pl.ANY)] * 7,
        out_shape=(
            jax.ShapeDtypeStruct((2 * HALF, WIDTH), BF16),
            jax.ShapeDtypeStruct((16, RUN, 2 * WIDTH), BF16),
        ),
        scratch_shapes=[
            pltpu.VMEM((RUN, HEADS * WIDTH), BF16),
            pltpu.VMEM((RUN, HEADS * WIDTH), BF16),
            pltpu.VMEM((RUN, HEADS * WIDTH), BF16),
            pltpu.VMEM((HEADS, RUN), F32),
            pltpu.VMEM((RUN, WIDTH), BF16),
            pltpu.VMEM((RUN, WIDTH), BF16),
            pltpu.VMEM((128, RUN), jnp.int32),
            pltpu.SemaphoreType.DMA((7,)),
        ],
        compiler_params=pltpu.CompilerParams(vmem_limit_bytes=60 * 1024 * 1024),
        name="prep",
    )(q, g, o, ln, k, v, pos)


def sorted_kernel(pos_ref, pay_ref, out_ref, copy_ref, qpt, kps, kx, vx):
    ylo, x, core, yhi, z = own_index()
    rows = []
    for key_yhi in range(2):
        for key_ylo in range(2):
            for key_x in range(4):
                rows.append(placed((key_ylo, key_x, core, key_yhi, z))[1])
    for query_core in (core, 1 - core):
        for query_z in (z, (z + 3) % 4, (z + 1) % 4, (z + 2) % 4):
            rows.append(placed((ylo, x, query_core, yhi, query_z))[0])
    pos = jnp.concatenate([pos_ref[pl.ds(row, 1), :] for row in rows], axis=0).astype(F32)
    rank = jnp.zeros_like(pos)
    for s in range(1, RUN):
        rank = rank + (pltpu.roll(pos, s, 1) < pos).astype(F32)
    lane = lax.broadcasted_iota(jnp.int32, pos.shape, 1).astype(F32)
    ordered = jnp.where(rank == lane, pos, 0.0)
    for s in range(1, RUN):
        ordered = ordered + jnp.where(
            pltpu.roll(rank, s, 1) == lane, pltpu.roll(pos, s, 1), 0.0
        )
    out_ref[...] = ordered
    copy_ref[...] = pay_ref[...]
    query_pos = jnp.concatenate(
        [ordered[KRUNS : KRUNS + QRUNS, :], jnp.zeros((RUN - QRUNS, RUN), F32)], axis=0
    ).T
    lane = lax.broadcasted_iota(jnp.int32, (BAND, WIDTH), 1)
    for band in range(BANDS):
        rows = slice(band * BAND, (band + 1) * BAND)
        kx[band] = ((lane % 8 == band) & (lane < 24)).astype(F32).astype(BF16)
        vx[band] = ((lane % 8 == band) & (lane >= 32) & (lane < 56)).astype(F32).astype(BF16)
        for run in range(QRUNS):
            qpt[band, run * BAND : (run + 1) * BAND, :] = jnp.broadcast_to(
                query_pos[rows, run : run + 1], (BAND, WIDTH)
            )
        kps[band : band + 1, :] = jnp.concatenate(
            [ordered[run : run + 1, rows] for run in range(KRUNS)], axis=1
        )


def sort_runs(pos, payload):
    return pl.pallas_call(
        sorted_kernel,
        out_shape=(
            jax.ShapeDtypeStruct((KRUNS + QRUNS, RUN), F32),
            jax.ShapeDtypeStruct(payload.shape, payload.dtype),
            jax.ShapeDtypeStruct((BANDS, QRUNS * BAND, WIDTH), F32),
            jax.ShapeDtypeStruct((BANDS, KROWS), F32),
            jax.ShapeDtypeStruct((BANDS, BAND, WIDTH), BF16),
            jax.ShapeDtypeStruct((BANDS, BAND, WIDTH), BF16),
        ),
        compiler_params=pltpu.CompilerParams(vmem_limit_bytes=32 * 1024 * 1024),
        name="sort_runs",
    )(pos, payload)


def main_kernel(*refs):
    spos, qpt, kps, kx, vx = refs[:5]
    runs = []
    for core in range(2):
        near, left, right, far_q, far_g = refs[5 + core * 5 : 10 + core * 5]
        runs += [(near, near, HALF), (left, left, HALF), (right, right, HALF), (far_q, far_g, 0)]
    kv_ref = refs[15]
    dq_near, dq_own, dq_other, dkv_ref = refs[16:20]
    dqs, dks, dvs, tx = refs[20:]
    for run, (q_pay, g_pay, base) in enumerate(runs):
        terms = jnp.concatenate(
            [
                q_pay[1024:1056, :].astype(F32),
                g_pay[base + 1024 : base + 1056, :].astype(F32),
                jnp.zeros((RUN - 64, RUN), F32),
            ],
            axis=0,
        )
        tx[run * RUN : (run + 1) * RUN, :] = terms.T.astype(BF16)
    dks[...] = jnp.zeros_like(dks)
    dvs[...] = jnp.zeros_like(dvs)
    by_cols = (((1,), (1,)), ((), ()))
    by_rows = (((0,), (0,)), ((), ()))

    def block(u, first, bands):
        at = pl.ds(pl.multiple_of(u * RUN, RUN), RUN)
        q = jnp.concatenate([pay[at, :] for pay, _, _ in runs], axis=0)
        g = jnp.concatenate(
            [
                pay[pl.ds(pl.multiple_of(base + u * RUN, 16), RUN), :]
                for _, pay, base in runs
            ],
            axis=0,
        )
        terms = tx[...]
        rows = [
            pl.ds(pl.multiple_of((first + i) * BAND, BAND), BAND) for i in range(bands)
        ]
        key = jnp.concatenate(
            [kv_ref[run, r, :WIDTH] for r in rows for run in range(KRUNS)], axis=0
        )
        value = jnp.concatenate(
            [kv_ref[run, r, WIDTH:] for r in rows for run in range(KRUNS)], axis=0
        )
        key_pick = jnp.concatenate([kx[u]] * (KRUNS * bands), axis=0)
        value_pick = jnp.concatenate([vx[u]] * (KRUNS * bands), axis=0)
        q_terms = jnp.concatenate([q, terms], axis=1)
        g_terms = jnp.concatenate([g, terms], axis=1)
        key_terms = jnp.concatenate([key, key_pick], axis=1)
        value_terms = jnp.concatenate([value, value_pick], axis=1)
        wide = KROWS * bands
        key_pos = jnp.concatenate([kps[pl.ds(first + i, 1), :] for i in range(bands)], axis=1)
        probs_low, grads_low = [], []
        for part in range(QROWS // PART):
            mine = slice(part * PART, (part + 1) * PART)
            lows = []
            for c in range(0, wide, PCOL):
                cs = slice(c, c + PCOL)
                scores = lax.dot_general(
                    q_terms[mine], key_terms[cs], by_cols, preferred_element_type=F32
                )
                grad_probs = lax.dot_general(
                    g_terms[mine], value_terms[cs], by_cols, preferred_element_type=F32
                )
                column = jnp.concatenate(
                    [
                        qpt[u, run * BAND : (run + 1) * BAND, :]
                        for run in range(part * PART // RUN, ((part + 1) * PART + RUN - 1) // RUN)
                        for _ in range(min(PART, RUN) // BAND)
                    ],
                    axis=0,
                )
                visible = key_pos[:, cs] <= jnp.concatenate([column] * (PCOL // WIDTH), axis=1)
                probs = jnp.where(visible, jnp.exp2(scores * (INV_ROOT * LOG2E)), 0.0)
                lows.append((probs.astype(BF16), (probs * grad_probs).astype(BF16)))
            probs_low.append(jnp.concatenate([x[0] for x in lows], axis=1))
            grads_low.append(jnp.concatenate([x[1] for x in lows], axis=1))
        probs_low = jnp.concatenate(probs_low, axis=0)
        grad_scores = jnp.concatenate(grads_low, axis=0)
        dv = lax.dot_general(g, probs_low, by_rows, preferred_element_type=F32)
        dk = lax.dot_general(q, grad_scores, by_rows, preferred_element_type=F32)
        for i in range(bands):
            cols = slice(i * KROWS, (i + 1) * KROWS)
            dvs[first + i] += dv[:, cols]
            dks[first + i] += dk[:, cols]
        dqs[...] += jnp.dot(grad_scores, key, preferred_element_type=F32)

    def query_band(u, carry):
        last = spos[KRUNS, u * BAND + BAND - 1]
        for run in range(1, QRUNS):
            last = jnp.maximum(last, spos[KRUNS + run, u * BAND + BAND - 1])
        seen = 0
        for t in range(BANDS):
            first = spos[0, t * BAND]
            for run in range(1, KRUNS):
                first = jnp.minimum(first, spos[run, t * BAND])
            seen = seen + jnp.where(last >= first, 1, 0)
        dqs[...] = jnp.zeros_like(dqs)
        done = lax.div(seen, MERGE) * MERGE

        def many(j, carry):
            block(u, j * MERGE, MERGE)
            return carry

        lax.fori_loop(0, lax.div(seen, MERGE), many, 0)

        def single(j, carry):
            block(u, j, 1)
            return carry

        lax.fori_loop(done, seen, single, 0)
        rows = pl.ds(pl.multiple_of(u * RUN, RUN), RUN)
        dq_near[rows, :] = dqs[0:RUN, :] * INV_ROOT
        for run in range(1, 4):
            dq_own[run - 1, rows, :] = (
                dqs[run * RUN : (run + 1) * RUN, :] * INV_ROOT
            ).astype(BF16)
        for run in range(4):
            dq_other[run, rows, :] = (
                dqs[(4 + run) * RUN : (5 + run) * RUN, :] * INV_ROOT
            ).astype(BF16)
        return carry

    lax.fori_loop(0, BANDS, query_band, 0)
    for band in range(BANDS):
        rows = slice(band * BAND, (band + 1) * BAND)
        key_part = (dks[band] * INV_ROOT).T.astype(BF16)
        value_part = dvs[band].T.astype(BF16)
        for run in range(KRUNS):
            dkv_ref[run, rows, :WIDTH] = key_part[run * BAND : (run + 1) * BAND]
            dkv_ref[run, rows, WIDTH:] = value_part[run * BAND : (run + 1) * BAND]


def main(runs, tables, payloads, kv):
    vmem = pl.BlockSpec(memory_space=pltpu.VMEM)
    return pl.pallas_call(
        main_kernel,
        in_specs=[pl.BlockSpec(memory_space=pltpu.SMEM)] + [vmem] * 15,
        out_shape=(
            jax.ShapeDtypeStruct((1024, WIDTH), F32),
            jax.ShapeDtypeStruct((3, 1024, WIDTH), BF16),
            jax.ShapeDtypeStruct((4, 1024, WIDTH), BF16),
            jax.ShapeDtypeStruct((16, RUN, 2 * WIDTH), BF16),
        ),
        scratch_shapes=[
            pltpu.VMEM((QROWS, WIDTH), F32),
            pltpu.VMEM((BANDS, WIDTH, KROWS), F32),
            pltpu.VMEM((BANDS, WIDTH, KROWS), F32),
            pltpu.VMEM((QROWS, WIDTH), BF16),
        ],
        compiler_params=pltpu.CompilerParams(vmem_limit_bytes=56 * 1024 * 1024),
        name="block_grads",
    )(runs, *tables, *payloads, kv)


def add_kernel(own_ref, in_ref, *out_refs):
    for run, out_ref in enumerate(out_refs):
        out_ref[...] = (own_ref[run].astype(F32) + in_ref[run + 1].astype(F32)).astype(BF16)


def final_kernel(
    own_ref, in_ref, b_ref, c_ref, d_ref, parts_ref, pos_ref, dq_ref, dk_ref, dv_ref
):
    q_block, k_block = placed(own_index())
    place, _ = rank_matrices(pos_ref[pl.ds(q_block, 1), :].astype(F32))
    total = own_ref[...] + in_ref[0].astype(F32)
    for ref in (b_ref, c_ref, d_ref):
        total = total + ref[...].astype(F32)
    total = total.reshape(BANDS, HEADS, BAND, WIDTH)
    for h in range(HEADS):
        dq_ref[:, h * WIDTH : (h + 1) * WIDTH] = lax.dot_general(
            place, total[:, h].reshape(RUN, WIDTH), (((0,), (0,)), ((), ())),
            precision=HIGH, preferred_element_type=F32,
        )
    place, _ = rank_matrices(pos_ref[pl.ds(k_block, 1), :].astype(F32))
    total = parts_ref[0].astype(F32)
    for i in range(1, 16):
        total = total + parts_ref[i].astype(F32)
    result = lax.dot_general(
        place, total, (((0,), (0,)), ((), ())), precision=HIGH, preferred_element_type=F32
    )
    dk_ref[...] = result[:, :WIDTH]
    dv_ref[...] = result[:, WIDTH:]


def shards(queries, key_rows, value_rows, output, out_grad, log_norm, positions):
    pos = positions.reshape(128, RUN)
    payload, kv_out = prep(queries, out_grad, output, log_norm, key_rows, value_rows, pos)

    def along_z(array, step):
        return lax.ppermute(array, "z", [(i, (i + step) % 4) for i in range(4)])

    def cross(array):
        return lax.ppermute(array, "core", [(0, 1), (1, 0)])

    from_left = along_z(payload, 1)
    from_right = along_z(payload, 3)
    far_q = along_z(from_left[:HALF], 1)
    far_g = along_z(from_right[HALF:], 3)
    mine = (payload, from_left, from_right, far_q, far_g)
    runs, handed, *tables = sort_runs(pos, payload)
    payloads = mine + (cross(handed),) + tuple(cross(array) for array in mine[1:])
    kv = lax.all_to_all(kv_out, PLANE, 0, 0, tiled=True)
    dq_near, dq_own, dq_other, dkv = main(runs, tables, payloads, kv)
    dkv_parts = lax.all_to_all(dkv, PLANE, 0, 0, tiled=True)
    dq_in = cross(dq_other)
    sums = pl.pallas_call(
        add_kernel,
        out_shape=[jax.ShapeDtypeStruct((1024, WIDTH), BF16)] * 3,
        compiler_params=pltpu.CompilerParams(vmem_limit_bytes=32 * 1024 * 1024),
        name="core_sum",
    )(dq_own, dq_in)
    dq_left = along_z(sums[0], 3)
    dq_right = along_z(sums[1], 1)
    dq_far = along_z(sums[2], 2)
    return pl.pallas_call(
        final_kernel,
        out_shape=(
            jax.ShapeDtypeStruct((RUN, HEADS * WIDTH), F32),
            jax.ShapeDtypeStruct((RUN, WIDTH), F32),
            jax.ShapeDtypeStruct((RUN, WIDTH), F32),
        ),
        compiler_params=pltpu.CompilerParams(vmem_limit_bytes=32 * 1024 * 1024),
        name="final_sums",
    )(dq_near, dq_in, dq_left, dq_right, dq_far, dkv_parts, pos)


def solution(mesh):
    fine = Mesh(mesh.devices.reshape(SIZES), AXES)
    by_query = P(AXES, None)
    by_key = P(("yhi", "z", "ylo", "x", "core"), None)
    return jax.shard_map(
        shards,
        mesh=fine,
        in_specs=(by_query, by_key, by_key, by_query, by_query, P(None, AXES), P()),
        out_specs=(by_query, by_key, by_key),
        check_vma=False,
    )
```

```python
import math

import jax
import jax.numpy as jnp
from jax import lax
from jax.experimental import pallas as pl
from jax.experimental.pallas import tpu as pltpu
from jax.sharding import Mesh, PartitionSpec as P

AXES = ("ylo", "x", "core", "yhi", "z")
SIZES = (2, 4, 2, 2, 4)
PLANE = ("yhi", "ylo", "x")
HEADS = 8
WIDTH = 128
RUN = 128
BAND = 16
BANDS = RUN // BAND
QRUNS = 8
KRUNS = 16
QROWS = QRUNS * BAND * HEADS
KROWS = KRUNS * BAND
MERGE = 4
PART = 256
PCOL = 256
HALF = 1024 + 32
LOG2E = math.log2(math.e)
INV_ROOT = 1.0 / math.sqrt(WIDTH)
F32 = jnp.float32
BF16 = jnp.bfloat16
HIGH = lax.Precision.HIGHEST


def rank_matrices(pos_row):
    by_lane = jnp.broadcast_to(pos_row, (RUN, RUN))
    by_row = by_lane.T
    rank_lane = jnp.sum((by_row < by_lane).astype(F32), axis=0, keepdims=True)
    row_id = lax.broadcasted_iota(jnp.int32, (RUN, RUN), 0).astype(F32)
    place = (rank_lane == row_id).astype(F32)
    return place, rank_lane


def split3(x):
    hi = x.astype(BF16)
    rest = x - hi.astype(F32)
    mid = rest.astype(BF16)
    low = (rest - mid.astype(F32)).astype(BF16)
    return hi, mid, low


def pack_rows(values, place, rank_lane):
    ordered = lax.dot_general(
        values, place, (((1,), (1,)), ((), ())), precision=HIGH, preferred_element_type=F32
    )
    pieces = []
    for band in range(BANDS):
        row = jnp.concatenate(
            [ordered[h : h + 1, band * BAND : (band + 1) * BAND] for h in range(HEADS)], axis=1
        )
        pieces.append(row)
    return jnp.concatenate(pieces, axis=0)


def placed(index):
    ylo, x, core, yhi, z = index
    pb = (ylo * 4 + x) * 2 + core
    return pb * 8 + yhi * 4 + z, (yhi * 4 + z) * 16 + pb


def own_index():
    return tuple(lax.axis_index(name) for name in AXES)


def prep_kernel(
    q_hbm, g_hbm, o_hbm, ln_hbm, k_hbm, v_hbm, pos_hbm, pay_ref, kv_ref,
    q_ref, g_ref, o_ref, ln_ref, k_ref, v_ref, pos_ref, sems,
):
    copies = [
        pltpu.make_async_copy(src, dst, sems.at[i])
        for i, (src, dst) in enumerate((
            (pos_hbm, pos_ref), (k_hbm, k_ref), (v_hbm, v_ref), (q_hbm, q_ref),
            (g_hbm, g_ref), (o_hbm, o_ref), (ln_hbm, ln_ref),
        ))
    ]
    for copy in copies:
        copy.start()
    copies[0].wait()
    q_block, k_block = placed(own_index())
    place_q, rank_q = rank_matrices(pos_ref[pl.ds(q_block, 1), :].astype(F32))
    place_k, _ = rank_matrices(pos_ref[pl.ds(k_block, 1), :].astype(F32))
    low_q = place_q.astype(BF16)
    low_k = place_k.astype(BF16)
    copies[1].wait()
    copies[2].wait()
    k_sorted = jnp.dot(low_k, k_ref[...], preferred_element_type=F32).astype(BF16)
    v_sorted = jnp.dot(low_k, v_ref[...], preferred_element_type=F32).astype(BF16)
    kv = jnp.concatenate([k_sorted, v_sorted], axis=1)
    for i in range(16):
        kv_ref[i] = kv
    copies[3].wait()
    q_sorted = jnp.dot(low_q, q_ref[...], preferred_element_type=F32).astype(BF16)
    copies[4].wait()
    g_sorted = jnp.dot(low_q, g_ref[...], preferred_element_type=F32).astype(BF16)
    for h in range(HEADS):
        for band in range(BANDS):
            at = (band * HEADS + h) * BAND
            rows = slice(band * BAND, (band + 1) * BAND)
            cols = slice(h * WIDTH, (h + 1) * WIDTH)
            pay_ref[at : at + BAND, :] = q_sorted[rows, cols]
            pay_ref[HALF + at : HALF + at + BAND, :] = g_sorted[rows, cols]
    copies[5].wait()
    copies[6].wait()
    product = g_ref[...].astype(F32) * o_ref[...].astype(F32)
    columns = [
        jnp.sum(product[:, h * WIDTH : (h + 1) * WIDTH], axis=1, keepdims=True)
        for h in range(HEADS)
    ]
    lane_id = lax.broadcasted_iota(jnp.int32, (RUN, RUN), 1)
    delta_wide = jnp.zeros((RUN, RUN), F32)
    for h in range(HEADS):
        delta_wide = jnp.where(lane_id == h, columns[h], delta_wide)
    delta = delta_wide.T[:HEADS]
    fill = jnp.zeros((BANDS, RUN), BF16)
    ln_hi, ln_mid, ln_low = split3(pack_rows(ln_ref[...] * (-1.0 / INV_ROOT), place_q, rank_q))
    pay_ref[1024:1056, :] = jnp.concatenate([ln_hi, ln_mid, ln_low, fill], axis=0)
    d_hi, d_mid, d_low = split3(pack_rows(-delta, place_q, rank_q))
    pay_ref[HALF + 1024 : HALF + 1056, :] = jnp.concatenate([d_hi, d_mid, d_low, fill], axis=0)


def prep(q, g, o, ln, k, v, pos):
    return pl.pallas_call(
        prep_kernel,
        in_specs=[pl.BlockSpec(memory_space=pl.ANY)] * 7,
        out_shape=(
            jax.ShapeDtypeStruct((2 * HALF, WIDTH), BF16),
            jax.ShapeDtypeStruct((16, RUN, 2 * WIDTH), BF16),
        ),
        scratch_shapes=[
            pltpu.VMEM((RUN, HEADS * WIDTH), BF16),
            pltpu.VMEM((RUN, HEADS * WIDTH), BF16),
            pltpu.VMEM((RUN, HEADS * WIDTH), BF16),
            pltpu.VMEM((HEADS, RUN), F32),
            pltpu.VMEM((RUN, WIDTH), BF16),
            pltpu.VMEM((RUN, WIDTH), BF16),
            pltpu.VMEM((128, RUN), jnp.int32),
            pltpu.SemaphoreType.DMA((7,)),
        ],
        compiler_params=pltpu.CompilerParams(vmem_limit_bytes=60 * 1024 * 1024),
        name="prep",
    )(q, g, o, ln, k, v, pos)


def sorted_kernel(pos_ref, pay_ref, seen_ref, copy_ref, qpt, kps, kx, vx):
    ylo, x, core, yhi, z = own_index()
    rows = []
    for key_yhi in range(2):
        for key_ylo in range(2):
            for key_x in range(4):
                rows.append(placed((key_ylo, key_x, core, key_yhi, z))[1])
    for query_core in (core, 1 - core):
        for query_z in (z, (z + 3) % 4, (z + 1) % 4, (z + 2) % 4):
            rows.append(placed((ylo, x, query_core, yhi, query_z))[0])
    pos = jnp.concatenate([pos_ref[pl.ds(row, 1), :] for row in rows], axis=0).astype(F32)
    rank = jnp.zeros_like(pos)
    for s in range(1, RUN):
        rank = rank + (pltpu.roll(pos, s, 1) < pos).astype(F32)
    lane = lax.broadcasted_iota(jnp.int32, pos.shape, 1).astype(F32)
    ordered = jnp.where(rank == lane, pos, 0.0)
    for s in range(1, RUN):
        ordered = ordered + jnp.where(
            pltpu.roll(rank, s, 1) == lane, pltpu.roll(pos, s, 1), 0.0
        )
    first = jnp.min(ordered[:KRUNS], axis=0, keepdims=True)
    last = jnp.max(ordered[KRUNS:], axis=0, keepdims=True)
    first = jnp.broadcast_to(first, (RUN, RUN)).T
    starts = lax.broadcasted_iota(jnp.int32, (RUN, RUN), 0) % BAND == 0
    seen = (starts & (first <= last)).astype(F32)
    seen_ref[...] = jnp.sum(seen, axis=0, keepdims=True).astype(jnp.int32)
    copy_ref[...] = pay_ref[...]
    query_pos = jnp.concatenate(
        [ordered[KRUNS : KRUNS + QRUNS, :], jnp.zeros((RUN - QRUNS, RUN), F32)], axis=0
    ).T
    lane = lax.broadcasted_iota(jnp.int32, (BAND, WIDTH), 1)
    for band in range(BANDS):
        rows = slice(band * BAND, (band + 1) * BAND)
        kx[band] = ((lane % 8 == band) & (lane < 24)).astype(F32).astype(BF16)
        vx[band] = ((lane % 8 == band) & (lane >= 32) & (lane < 56)).astype(F32).astype(BF16)
        for run in range(QRUNS):
            qpt[band, run * BAND : (run + 1) * BAND, :] = jnp.broadcast_to(
                query_pos[rows, run : run + 1], (BAND, WIDTH)
            )
        kps[band : band + 1, :] = jnp.concatenate(
            [ordered[run : run + 1, rows] for run in range(KRUNS)], axis=1
        )


def sort_runs(pos, payload):
    return pl.pallas_call(
        sorted_kernel,
        out_shape=(
            jax.ShapeDtypeStruct((1, RUN), jnp.int32),
            jax.ShapeDtypeStruct(payload.shape, payload.dtype),
            jax.ShapeDtypeStruct((BANDS, QRUNS * BAND, WIDTH), F32),
            jax.ShapeDtypeStruct((BANDS, KROWS), F32),
            jax.ShapeDtypeStruct((BANDS, BAND, WIDTH), BF16),
            jax.ShapeDtypeStruct((BANDS, BAND, WIDTH), BF16),
        ),
        compiler_params=pltpu.CompilerParams(vmem_limit_bytes=32 * 1024 * 1024),
        name="sort_runs",
    )(pos, payload)


def main_kernel(*refs):
    counts, qpt, kps, kx, vx = refs[:5]
    runs = []
    for core in range(2):
        near, left, right, far_q, far_g = refs[5 + core * 5 : 10 + core * 5]
        runs += [(near, near, HALF), (left, left, HALF), (right, right, HALF), (far_q, far_g, 0)]
    kv_ref = refs[15]
    dq_near, dq_own, dq_other, dkv_ref = refs[16:20]
    dqs, dks, dvs, tx = refs[20:]
    for run, (q_pay, g_pay, base) in enumerate(runs):
        terms = jnp.concatenate(
            [
                q_pay[1024:1056, :].astype(F32),
                g_pay[base + 1024 : base + 1056, :].astype(F32),
                jnp.zeros((RUN - 64, RUN), F32),
            ],
            axis=0,
        )
        tx[run * RUN : (run + 1) * RUN, :] = terms.T.astype(BF16)
    dks[...] = jnp.zeros_like(dks)
    dvs[...] = jnp.zeros_like(dvs)
    by_cols = (((1,), (1,)), ((), ()))
    by_rows = (((0,), (0,)), ((), ()))

    def block(u, first, bands):
        at = pl.ds(pl.multiple_of(u * RUN, RUN), RUN)
        q = jnp.concatenate([pay[at, :] for pay, _, _ in runs], axis=0)
        g = jnp.concatenate(
            [
                pay[pl.ds(pl.multiple_of(base + u * RUN, 16), RUN), :]
                for _, pay, base in runs
            ],
            axis=0,
        )
        terms = tx[...]
        rows = [
            pl.ds(pl.multiple_of((first + i) * BAND, BAND), BAND) for i in range(bands)
        ]
        key = jnp.concatenate(
            [kv_ref[run, r, :WIDTH] for r in rows for run in range(KRUNS)], axis=0
        )
        value = jnp.concatenate(
            [kv_ref[run, r, WIDTH:] for r in rows for run in range(KRUNS)], axis=0
        )
        key_pick = jnp.concatenate([kx[u]] * (KRUNS * bands), axis=0)
        value_pick = jnp.concatenate([vx[u]] * (KRUNS * bands), axis=0)
        q_terms = jnp.concatenate([q, terms], axis=1)
        g_terms = jnp.concatenate([g, terms], axis=1)
        key_terms = jnp.concatenate([key, key_pick], axis=1)
        value_terms = jnp.concatenate([value, value_pick], axis=1)
        wide = KROWS * bands
        key_pos = jnp.concatenate([kps[pl.ds(first + i, 1), :] for i in range(bands)], axis=1)
        probs_low, grads_low = [], []
        for part in range(QROWS // PART):
            mine = slice(part * PART, (part + 1) * PART)
            lows = []
            for c in range(0, wide, PCOL):
                cs = slice(c, c + PCOL)
                scores = lax.dot_general(
                    q_terms[mine], key_terms[cs], by_cols, preferred_element_type=F32
                )
                grad_probs = lax.dot_general(
                    g_terms[mine], value_terms[cs], by_cols, preferred_element_type=F32
                )
                column = jnp.concatenate(
                    [
                        qpt[u, run * BAND : (run + 1) * BAND, :]
                        for run in range(part * PART // RUN, ((part + 1) * PART + RUN - 1) // RUN)
                        for _ in range(min(PART, RUN) // BAND)
                    ],
                    axis=0,
                )
                visible = key_pos[:, cs] <= jnp.concatenate([column] * (PCOL // WIDTH), axis=1)
                probs = jnp.where(visible, jnp.exp2(scores * (INV_ROOT * LOG2E)), 0.0)
                lows.append((probs.astype(BF16), (probs * grad_probs).astype(BF16)))
            probs_low.append(jnp.concatenate([x[0] for x in lows], axis=1))
            grads_low.append(jnp.concatenate([x[1] for x in lows], axis=1))
        probs_low = jnp.concatenate(probs_low, axis=0)
        grad_scores = jnp.concatenate(grads_low, axis=0)
        dv = lax.dot_general(g, probs_low, by_rows, preferred_element_type=F32)
        dk = lax.dot_general(q, grad_scores, by_rows, preferred_element_type=F32)
        for i in range(bands):
            cols = slice(i * KROWS, (i + 1) * KROWS)
            dvs[first + i] += dv[:, cols]
            dks[first + i] += dk[:, cols]
        dqs[...] += jnp.dot(grad_scores, key, preferred_element_type=F32)

    def query_band(u, carry):
        seen = counts[0, u * BAND + BAND - 1]
        dqs[...] = jnp.zeros_like(dqs)
        done = lax.div(seen, MERGE) * MERGE

        def many(j, carry):
            block(u, j * MERGE, MERGE)
            return carry

        lax.fori_loop(0, lax.div(seen, MERGE), many, 0)

        def single(j, carry):
            block(u, j, 1)
            return carry

        lax.fori_loop(done, seen, single, 0)
        rows = pl.ds(pl.multiple_of(u * RUN, RUN), RUN)
        dq_near[rows, :] = dqs[0:RUN, :] * INV_ROOT
        for run in range(1, 4):
            dq_own[run - 1, rows, :] = (
                dqs[run * RUN : (run + 1) * RUN, :] * INV_ROOT
            ).astype(BF16)
        for run in range(4):
            dq_other[run, rows, :] = (
                dqs[(4 + run) * RUN : (5 + run) * RUN, :] * INV_ROOT
            ).astype(BF16)
        return carry

    lax.fori_loop(0, BANDS, query_band, 0)
    for band in range(BANDS):
        rows = slice(band * BAND, (band + 1) * BAND)
        key_part = (dks[band] * INV_ROOT).T.astype(BF16)
        value_part = dvs[band].T.astype(BF16)
        for run in range(KRUNS):
            dkv_ref[run, rows, :WIDTH] = key_part[run * BAND : (run + 1) * BAND]
            dkv_ref[run, rows, WIDTH:] = value_part[run * BAND : (run + 1) * BAND]


def main(counts, tables, payloads, kv):
    vmem = pl.BlockSpec(memory_space=pltpu.VMEM)
    return pl.pallas_call(
        main_kernel,
        in_specs=[pl.BlockSpec(memory_space=pltpu.SMEM)] + [vmem] * 15,
        out_shape=(
            jax.ShapeDtypeStruct((1024, WIDTH), F32),
            jax.ShapeDtypeStruct((3, 1024, WIDTH), BF16),
            jax.ShapeDtypeStruct((4, 1024, WIDTH), BF16),
            jax.ShapeDtypeStruct((16, RUN, 2 * WIDTH), BF16),
        ),
        scratch_shapes=[
            pltpu.VMEM((QROWS, WIDTH), F32),
            pltpu.VMEM((BANDS, WIDTH, KROWS), F32),
            pltpu.VMEM((BANDS, WIDTH, KROWS), F32),
            pltpu.VMEM((QROWS, WIDTH), BF16),
        ],
        compiler_params=pltpu.CompilerParams(vmem_limit_bytes=56 * 1024 * 1024),
        name="block_grads",
    )(counts, *tables, *payloads, kv)


def add_kernel(own_ref, in_ref, *out_refs):
    for run, out_ref in enumerate(out_refs):
        out_ref[...] = (own_ref[run].astype(F32) + in_ref[run + 1].astype(F32)).astype(BF16)


def final_kernel(
    own_ref, in_ref, b_ref, c_ref, d_ref, parts_ref, pos_ref, dq_ref, dk_ref, dv_ref
):
    q_block, k_block = placed(own_index())
    place, _ = rank_matrices(pos_ref[pl.ds(q_block, 1), :].astype(F32))
    total = own_ref[...] + in_ref[0].astype(F32)
    for ref in (b_ref, c_ref, d_ref):
        total = total + ref[...].astype(F32)
    total = total.reshape(BANDS, HEADS, BAND, WIDTH)
    for h in range(HEADS):
        dq_ref[:, h * WIDTH : (h + 1) * WIDTH] = lax.dot_general(
            place, total[:, h].reshape(RUN, WIDTH), (((0,), (0,)), ((), ())),
            precision=HIGH, preferred_element_type=F32,
        )
    place, _ = rank_matrices(pos_ref[pl.ds(k_block, 1), :].astype(F32))
    total = parts_ref[0].astype(F32)
    for i in range(1, 16):
        total = total + parts_ref[i].astype(F32)
    result = lax.dot_general(
        place, total, (((0,), (0,)), ((), ())), precision=HIGH, preferred_element_type=F32
    )
    dk_ref[...] = result[:, :WIDTH]
    dv_ref[...] = result[:, WIDTH:]


def shards(queries, key_rows, value_rows, output, out_grad, log_norm, positions):
    pos = positions.reshape(128, RUN)
    payload, kv_out = prep(queries, out_grad, output, log_norm, key_rows, value_rows, pos)

    def along_z(array, step):
        return lax.ppermute(array, "z", [(i, (i + step) % 4) for i in range(4)])

    def cross(array):
        return lax.ppermute(array, "core", [(0, 1), (1, 0)])

    from_left = along_z(payload, 1)
    from_right = along_z(payload, 3)
    far_q = along_z(from_left[:HALF], 1)
    far_g = along_z(from_right[HALF:], 3)
    mine = (payload, from_left, from_right, far_q, far_g)
    counts, handed, *tables = sort_runs(pos, payload)
    payloads = mine + (cross(handed),) + tuple(cross(array) for array in mine[1:])
    kv = lax.all_to_all(kv_out, PLANE, 0, 0, tiled=True)
    dq_near, dq_own, dq_other, dkv = main(counts, tables, payloads, kv)
    dkv_parts = lax.all_to_all(dkv, PLANE, 0, 0, tiled=True)
    dq_in = cross(dq_other)
    sums = pl.pallas_call(
        add_kernel,
        out_shape=[jax.ShapeDtypeStruct((1024, WIDTH), BF16)] * 3,
        compiler_params=pltpu.CompilerParams(vmem_limit_bytes=32 * 1024 * 1024),
        name="core_sum",
    )(dq_own, dq_in)
    dq_left = along_z(sums[0], 3)
    dq_right = along_z(sums[1], 1)
    dq_far = along_z(sums[2], 2)
    return pl.pallas_call(
        final_kernel,
        out_shape=(
            jax.ShapeDtypeStruct((RUN, HEADS * WIDTH), F32),
            jax.ShapeDtypeStruct((RUN, WIDTH), F32),
            jax.ShapeDtypeStruct((RUN, WIDTH), F32),
        ),
        compiler_params=pltpu.CompilerParams(vmem_limit_bytes=32 * 1024 * 1024),
        name="final_sums",
    )(dq_near, dq_in, dq_left, dq_right, dq_far, dkv_parts, pos)


def solution(mesh):
    fine = Mesh(mesh.devices.reshape(SIZES), AXES)
    by_query = P(AXES, None)
    by_key = P(("yhi", "z", "ylo", "x", "core"), None)
    return jax.shard_map(
        shards,
        mesh=fine,
        in_specs=(by_query, by_key, by_key, by_query, by_query, P(None, AXES), P()),
        out_specs=(by_query, by_key, by_key),
        check_vma=False,
    )
```

```python
import math

import jax
import jax.numpy as jnp
from jax import lax
from jax.experimental import pallas as pl
from jax.experimental.pallas import tpu as pltpu
from jax.sharding import Mesh, PartitionSpec as P

AXES = ("ylo", "x", "core", "yhi", "z")
SIZES = (2, 4, 2, 2, 4)
PLANE = ("yhi", "ylo", "x")
HEADS = 8
WIDTH = 128
RUN = 128
BAND = 16
BANDS = RUN // BAND
QRUNS = 8
KRUNS = 16
QROWS = QRUNS * BAND * HEADS
KROWS = KRUNS * BAND
MERGE = 4
PART = 256
PCOL = 256
HALF = 1024 + 32
LOG2E = math.log2(math.e)
INV_ROOT = 1.0 / math.sqrt(WIDTH)
F32 = jnp.float32
BF16 = jnp.bfloat16
HIGH = lax.Precision.HIGHEST


def rank_matrices(pos_row):
    by_lane = jnp.broadcast_to(pos_row, (RUN, RUN))
    by_row = by_lane.T
    rank_lane = jnp.sum((by_row < by_lane).astype(F32), axis=0, keepdims=True)
    row_id = lax.broadcasted_iota(jnp.int32, (RUN, RUN), 0).astype(F32)
    place = (rank_lane == row_id).astype(F32)
    return place, rank_lane


def split3(x):
    hi = x.astype(BF16)
    rest = x - hi.astype(F32)
    mid = rest.astype(BF16)
    low = (rest - mid.astype(F32)).astype(BF16)
    return hi, mid, low


def pack_rows(values, place, rank_lane):
    ordered = lax.dot_general(
        values, place, (((1,), (1,)), ((), ())), precision=HIGH, preferred_element_type=F32
    )
    row = lax.broadcasted_iota(jnp.int32, (BANDS, RUN), 0)
    piece = lax.broadcasted_iota(jnp.int32, (BANDS, RUN), 1) // BAND
    turned = jnp.zeros((BANDS, RUN), F32)
    for s in range(BANDS):
        moved = ordered if s == 0 else pltpu.roll(pltpu.roll(ordered, BAND * s, 1), BANDS - s, 0)
        turned = jnp.where(piece == (row + s) % BANDS, moved, turned)
    return turned


def unsort(place, rows):
    back = place.T.astype(BF16)
    low, mid, high = (
        jnp.dot(back, part, preferred_element_type=F32) for part in split3(rows)[::-1]
    )
    return (low + mid) + high


def placed(index):
    ylo, x, core, yhi, z = index
    pb = (ylo * 4 + x) * 2 + core
    return pb * 8 + yhi * 4 + z, (yhi * 4 + z) * 16 + pb


def own_index():
    return tuple(lax.axis_index(name) for name in AXES)


def prep_kernel(
    q_hbm, g_hbm, o_hbm, ln_hbm, k_hbm, v_hbm, pos_hbm, pay_ref, kv_ref,
    q_ref, g_ref, o_ref, ln_ref, k_ref, v_ref, pos_ref, sems,
):
    copies = [
        pltpu.make_async_copy(src, dst, sems.at[i])
        for i, (src, dst) in enumerate((
            (pos_hbm, pos_ref), (k_hbm, k_ref), (v_hbm, v_ref), (q_hbm, q_ref),
            (g_hbm, g_ref), (o_hbm, o_ref), (ln_hbm, ln_ref),
        ))
    ]
    for copy in copies:
        copy.start()
    copies[0].wait()
    q_block, k_block = placed(own_index())
    place_q, rank_q = rank_matrices(pos_ref[pl.ds(q_block, 1), :].astype(F32))
    place_k, _ = rank_matrices(pos_ref[pl.ds(k_block, 1), :].astype(F32))
    low_q = place_q.astype(BF16)
    low_k = place_k.astype(BF16)
    copies[1].wait()
    copies[2].wait()
    k_sorted = jnp.dot(low_k, k_ref[...], preferred_element_type=F32).astype(BF16)
    v_sorted = jnp.dot(low_k, v_ref[...], preferred_element_type=F32).astype(BF16)
    kv = jnp.concatenate([k_sorted, v_sorted], axis=1)
    for i in range(16):
        kv_ref[i] = kv
    copies[3].wait()
    q_sorted = jnp.dot(low_q, q_ref[...], preferred_element_type=F32).astype(BF16)
    copies[4].wait()
    g_sorted = jnp.dot(low_q, g_ref[...], preferred_element_type=F32).astype(BF16)
    for h in range(HEADS):
        for band in range(BANDS):
            at = (band * HEADS + h) * BAND
            rows = slice(band * BAND, (band + 1) * BAND)
            cols = slice(h * WIDTH, (h + 1) * WIDTH)
            pay_ref[at : at + BAND, :] = q_sorted[rows, cols]
            pay_ref[HALF + at : HALF + at + BAND, :] = g_sorted[rows, cols]
    copies[5].wait()
    copies[6].wait()
    product = g_ref[...].astype(F32) * o_ref[...].astype(F32)
    columns = [
        jnp.sum(product[:, h * WIDTH : (h + 1) * WIDTH], axis=1, keepdims=True)
        for h in range(HEADS)
    ]
    lane_id = lax.broadcasted_iota(jnp.int32, (RUN, RUN), 1)
    delta_wide = jnp.zeros((RUN, RUN), F32)
    for h in range(HEADS):
        delta_wide = jnp.where(lane_id == h, columns[h], delta_wide)
    delta = delta_wide.T[:HEADS]
    fill = jnp.zeros((BANDS, RUN), BF16)
    ln_hi, ln_mid, ln_low = split3(pack_rows(ln_ref[...] * (-1.0 / INV_ROOT), place_q, rank_q))
    pay_ref[1024:1056, :] = jnp.concatenate([ln_hi, ln_mid, ln_low, fill], axis=0)
    d_hi, d_mid, d_low = split3(pack_rows(-delta, place_q, rank_q))
    pay_ref[HALF + 1024 : HALF + 1056, :] = jnp.concatenate([d_hi, d_mid, d_low, fill], axis=0)


def prep(q, g, o, ln, k, v, pos):
    return pl.pallas_call(
        prep_kernel,
        in_specs=[pl.BlockSpec(memory_space=pl.ANY)] * 7,
        out_shape=(
            jax.ShapeDtypeStruct((2 * HALF, WIDTH), BF16),
            jax.ShapeDtypeStruct((16, RUN, 2 * WIDTH), BF16),
        ),
        scratch_shapes=[
            pltpu.VMEM((RUN, HEADS * WIDTH), BF16),
            pltpu.VMEM((RUN, HEADS * WIDTH), BF16),
            pltpu.VMEM((RUN, HEADS * WIDTH), BF16),
            pltpu.VMEM((HEADS, RUN), F32),
            pltpu.VMEM((RUN, WIDTH), BF16),
            pltpu.VMEM((RUN, WIDTH), BF16),
            pltpu.VMEM((128, RUN), jnp.int32),
            pltpu.SemaphoreType.DMA((7,)),
        ],
        compiler_params=pltpu.CompilerParams(vmem_limit_bytes=60 * 1024 * 1024),
        name="prep",
    )(q, g, o, ln, k, v, pos)


def sorted_kernel(pos_ref, pay_ref, seen_ref, copy_ref, qpt, kps, kx, vx):
    ylo, x, core, yhi, z = own_index()
    rows = []
    for key_yhi in range(2):
        for key_ylo in range(2):
            for key_x in range(4):
                rows.append(placed((key_ylo, key_x, core, key_yhi, z))[1])
    for query_core in (core, 1 - core):
        for query_z in (z, (z + 3) % 4, (z + 1) % 4, (z + 2) % 4):
            rows.append(placed((ylo, x, query_core, yhi, query_z))[0])
    pos = jnp.concatenate([pos_ref[pl.ds(row, 1), :] for row in rows], axis=0).astype(F32)
    rank = jnp.zeros_like(pos)
    for s in range(1, RUN):
        rank = rank + (pltpu.roll(pos, s, 1) < pos).astype(F32)
    lane = lax.broadcasted_iota(jnp.int32, pos.shape, 1).astype(F32)
    ordered = jnp.where(rank == lane, pos, 0.0)
    for s in range(1, RUN):
        ordered = ordered + jnp.where(
            pltpu.roll(rank, s, 1) == lane, pltpu.roll(pos, s, 1), 0.0
        )
    first = jnp.min(ordered[:KRUNS], axis=0, keepdims=True)
    last = jnp.max(ordered[KRUNS:], axis=0, keepdims=True)
    first = jnp.broadcast_to(first, (RUN, RUN)).T
    starts = lax.broadcasted_iota(jnp.int32, (RUN, RUN), 0) % BAND == 0
    seen = (starts & (first <= last)).astype(F32)
    seen_ref[...] = jnp.sum(seen, axis=0, keepdims=True).astype(jnp.int32)
    copy_ref[...] = pay_ref[...]
    query_pos = jnp.concatenate(
        [ordered[KRUNS : KRUNS + QRUNS, :], jnp.zeros((RUN - QRUNS, RUN), F32)], axis=0
    ).T
    lane = lax.broadcasted_iota(jnp.int32, (BAND, WIDTH), 1)
    for band in range(BANDS):
        rows = slice(band * BAND, (band + 1) * BAND)
        kx[band] = ((lane % 8 == band) & (lane < 24)).astype(F32).astype(BF16)
        vx[band] = ((lane % 8 == band) & (lane >= 32) & (lane < 56)).astype(F32).astype(BF16)
        for run in range(QRUNS):
            qpt[band, run * BAND : (run + 1) * BAND, :] = jnp.broadcast_to(
                query_pos[rows, run : run + 1], (BAND, WIDTH)
            )
        kps[band : band + 1, :] = jnp.concatenate(
            [ordered[run : run + 1, rows] for run in range(KRUNS)], axis=1
        )


def sort_runs(pos, payload):
    return pl.pallas_call(
        sorted_kernel,
        out_shape=(
            jax.ShapeDtypeStruct((1, RUN), jnp.int32),
            jax.ShapeDtypeStruct(payload.shape, payload.dtype),
            jax.ShapeDtypeStruct((BANDS, QRUNS * BAND, WIDTH), F32),
            jax.ShapeDtypeStruct((BANDS, KROWS), F32),
            jax.ShapeDtypeStruct((BANDS, BAND, WIDTH), BF16),
            jax.ShapeDtypeStruct((BANDS, BAND, WIDTH), BF16),
        ),
        compiler_params=pltpu.CompilerParams(vmem_limit_bytes=32 * 1024 * 1024),
        name="sort_runs",
    )(pos, payload)


def main_kernel(*refs):
    counts, qpt, kps, kx, vx = refs[:5]
    runs = []
    for core in range(2):
        near, left, right, far_q, far_g = refs[5 + core * 5 : 10 + core * 5]
        runs += [(near, near, HALF), (left, left, HALF), (right, right, HALF), (far_q, far_g, 0)]
    kv_ref = refs[15]
    dq_near, dq_own, dq_other, dkv_ref = refs[16:20]
    dqs, dks, dvs, tx = refs[20:]
    for run, (q_pay, g_pay, base) in enumerate(runs):
        terms = jnp.concatenate(
            [
                q_pay[1024:1056, :].astype(F32),
                g_pay[base + 1024 : base + 1056, :].astype(F32),
                jnp.zeros((RUN - 64, RUN), F32),
            ],
            axis=0,
        )
        tx[run * RUN : (run + 1) * RUN, :] = terms.T.astype(BF16)
    dks[...] = jnp.zeros_like(dks)
    dvs[...] = jnp.zeros_like(dvs)
    by_cols = (((1,), (1,)), ((), ()))
    by_rows = (((0,), (0,)), ((), ()))

    def block(u, first, bands):
        at = pl.ds(pl.multiple_of(u * RUN, RUN), RUN)
        q = jnp.concatenate([pay[at, :] for pay, _, _ in runs], axis=0)
        g = jnp.concatenate(
            [
                pay[pl.ds(pl.multiple_of(base + u * RUN, 16), RUN), :]
                for _, pay, base in runs
            ],
            axis=0,
        )
        terms = tx[...]
        rows = [
            pl.ds(pl.multiple_of((first + i) * BAND, BAND), BAND) for i in range(bands)
        ]
        key = jnp.concatenate(
            [kv_ref[run, r, :WIDTH] for r in rows for run in range(KRUNS)], axis=0
        )
        value = jnp.concatenate(
            [kv_ref[run, r, WIDTH:] for r in rows for run in range(KRUNS)], axis=0
        )
        key_pick = jnp.concatenate([kx[u]] * (KRUNS * bands), axis=0)
        value_pick = jnp.concatenate([vx[u]] * (KRUNS * bands), axis=0)
        q_terms = jnp.concatenate([q, terms], axis=1)
        g_terms = jnp.concatenate([g, terms], axis=1)
        key_terms = jnp.concatenate([key, key_pick], axis=1)
        value_terms = jnp.concatenate([value, value_pick], axis=1)
        wide = KROWS * bands
        key_pos = jnp.concatenate([kps[pl.ds(first + i, 1), :] for i in range(bands)], axis=1)
        probs_low, grads_low = [], []
        for part in range(QROWS // PART):
            mine = slice(part * PART, (part + 1) * PART)
            lows = []
            for c in range(0, wide, PCOL):
                cs = slice(c, c + PCOL)
                scores = lax.dot_general(
                    q_terms[mine], key_terms[cs], by_cols, preferred_element_type=F32
                )
                grad_probs = lax.dot_general(
                    g_terms[mine], value_terms[cs], by_cols, preferred_element_type=F32
                )
                column = jnp.concatenate(
                    [
                        qpt[u, run * BAND : (run + 1) * BAND, :]
                        for run in range(part * PART // RUN, ((part + 1) * PART + RUN - 1) // RUN)
                        for _ in range(min(PART, RUN) // BAND)
                    ],
                    axis=0,
                )
                visible = key_pos[:, cs] <= jnp.concatenate([column] * (PCOL // WIDTH), axis=1)
                probs = jnp.where(visible, jnp.exp2(scores * (INV_ROOT * LOG2E)), 0.0)
                lows.append((probs.astype(BF16), (probs * grad_probs).astype(BF16)))
            probs_low.append(jnp.concatenate([x[0] for x in lows], axis=1))
            grads_low.append(jnp.concatenate([x[1] for x in lows], axis=1))
        probs_low = jnp.concatenate(probs_low, axis=0)
        grad_scores = jnp.concatenate(grads_low, axis=0)
        dv = lax.dot_general(g, probs_low, by_rows, preferred_element_type=F32)
        dk = lax.dot_general(q, grad_scores, by_rows, preferred_element_type=F32)
        for i in range(bands):
            cols = slice(i * KROWS, (i + 1) * KROWS)
            dvs[first + i] += dv[:, cols]
            dks[first + i] += dk[:, cols]
        dqs[...] += jnp.dot(grad_scores, key, preferred_element_type=F32)

    def query_band(u, carry):
        seen = counts[0, u * BAND + BAND - 1]
        dqs[...] = jnp.zeros_like(dqs)
        done = lax.div(seen, MERGE) * MERGE

        def many(j, carry):
            block(u, j * MERGE, MERGE)
            return carry

        lax.fori_loop(0, lax.div(seen, MERGE), many, 0)

        def single(j, carry):
            block(u, j, 1)
            return carry

        lax.fori_loop(done, seen, single, 0)
        rows = pl.ds(pl.multiple_of(u * RUN, RUN), RUN)
        dq_near[rows, :] = dqs[0:RUN, :] * INV_ROOT
        for run in range(1, 4):
            dq_own[run - 1, rows, :] = (
                dqs[run * RUN : (run + 1) * RUN, :] * INV_ROOT
            ).astype(BF16)
        for run in range(4):
            dq_other[run, rows, :] = (
                dqs[(4 + run) * RUN : (5 + run) * RUN, :] * INV_ROOT
            ).astype(BF16)
        return carry

    lax.fori_loop(0, BANDS, query_band, 0)
    for band in range(BANDS):
        rows = slice(band * BAND, (band + 1) * BAND)
        key_part = (dks[band] * INV_ROOT).astype(BF16).T
        value_part = dvs[band].astype(BF16).T
        for run in range(KRUNS):
            dkv_ref[run, rows, :WIDTH] = key_part[run * BAND : (run + 1) * BAND]
            dkv_ref[run, rows, WIDTH:] = value_part[run * BAND : (run + 1) * BAND]


def main(counts, tables, payloads, kv):
    vmem = pl.BlockSpec(memory_space=pltpu.VMEM)
    return pl.pallas_call(
        main_kernel,
        in_specs=[pl.BlockSpec(memory_space=pltpu.SMEM)] + [vmem] * 15,
        out_shape=(
            jax.ShapeDtypeStruct((1024, WIDTH), F32),
            jax.ShapeDtypeStruct((3, 1024, WIDTH), BF16),
            jax.ShapeDtypeStruct((4, 1024, WIDTH), BF16),
            jax.ShapeDtypeStruct((16, RUN, 2 * WIDTH), BF16),
        ),
        scratch_shapes=[
            pltpu.VMEM((QROWS, WIDTH), F32),
            pltpu.VMEM((BANDS, WIDTH, KROWS), F32),
            pltpu.VMEM((BANDS, WIDTH, KROWS), F32),
            pltpu.VMEM((QROWS, WIDTH), BF16),
        ],
        compiler_params=pltpu.CompilerParams(vmem_limit_bytes=56 * 1024 * 1024),
        name="block_grads",
    )(counts, *tables, *payloads, kv)


def add_kernel(own_ref, in_ref, *out_refs):
    for run, out_ref in enumerate(out_refs):
        out_ref[...] = (own_ref[run].astype(F32) + in_ref[run + 1].astype(F32)).astype(BF16)


def final_kernel(
    own_ref, in_ref, b_ref, c_ref, d_ref, parts_ref, pos_ref, dq_ref, dk_ref, dv_ref
):
    q_block, k_block = placed(own_index())
    place, _ = rank_matrices(pos_ref[pl.ds(q_block, 1), :].astype(F32))
    total = own_ref[...] + in_ref[0].astype(F32)
    for ref in (b_ref, c_ref, d_ref):
        total = total + ref[...].astype(F32)
    total = total.reshape(BANDS, HEADS, BAND, WIDTH)
    dq_ref[...] = unsort(
        place, jnp.concatenate([total[:, h].reshape(RUN, WIDTH) for h in range(HEADS)], axis=1)
    )
    place, _ = rank_matrices(pos_ref[pl.ds(k_block, 1), :].astype(F32))
    total = parts_ref[0].astype(F32)
    for i in range(1, 16):
        total = total + parts_ref[i].astype(F32)
    result = unsort(place, total)
    dk_ref[...] = result[:, :WIDTH]
    dv_ref[...] = result[:, WIDTH:]


def shards(queries, key_rows, value_rows, output, out_grad, log_norm, positions):
    pos = positions.reshape(128, RUN)
    payload, kv_out = prep(queries, out_grad, output, log_norm, key_rows, value_rows, pos)

    def along_z(array, step):
        return lax.ppermute(array, "z", [(i, (i + step) % 4) for i in range(4)])

    def cross(array):
        return lax.ppermute(array, "core", [(0, 1), (1, 0)])

    from_left = along_z(payload, 1)
    from_right = along_z(payload, 3)
    far_q = along_z(from_left[:HALF], 1)
    far_g = along_z(from_right[HALF:], 3)
    mine = (payload, from_left, from_right, far_q, far_g)
    counts, handed, *tables = sort_runs(pos, payload)
    payloads = mine + (cross(handed),) + tuple(cross(array) for array in mine[1:])
    kv = lax.all_to_all(kv_out, PLANE, 0, 0, tiled=True)
    dq_near, dq_own, dq_other, dkv = main(counts, tables, payloads, kv)
    dkv_parts = lax.all_to_all(dkv, PLANE, 0, 0, tiled=True)
    dq_in = cross(dq_other)
    sums = pl.pallas_call(
        add_kernel,
        out_shape=[jax.ShapeDtypeStruct((1024, WIDTH), BF16)] * 3,
        compiler_params=pltpu.CompilerParams(vmem_limit_bytes=32 * 1024 * 1024),
        name="core_sum",
    )(dq_own, dq_in)
    dq_left = along_z(sums[0], 3)
    dq_right = along_z(sums[1], 1)
    dq_far = along_z(sums[2], 2)
    return pl.pallas_call(
        final_kernel,
        out_shape=(
            jax.ShapeDtypeStruct((RUN, HEADS * WIDTH), F32),
            jax.ShapeDtypeStruct((RUN, WIDTH), F32),
            jax.ShapeDtypeStruct((RUN, WIDTH), F32),
        ),
        compiler_params=pltpu.CompilerParams(vmem_limit_bytes=32 * 1024 * 1024),
        name="final_sums",
    )(dq_near, dq_in, dq_left, dq_right, dq_far, dkv_parts, pos)


def solution(mesh):
    fine = Mesh(mesh.devices.reshape(SIZES), AXES)
    by_query = P(AXES, None)
    by_key = P(("yhi", "z", "ylo", "x", "core"), None)
    return jax.shard_map(
        shards,
        mesh=fine,
        in_specs=(by_query, by_key, by_key, by_query, by_query, P(None, AXES), P()),
        out_specs=(by_query, by_key, by_key),
        check_vma=False,
    )
```
